32 devices in a mesh: frames: 8 (over y, x, core), pairs: 4 (over z).
Axes of the slice: x: 2, y: 2, z: 4, core: 2. Of those that a mesh axis runs over, the one named last changes fastest.
Arguments:
- coords: float32 [5120, 3, 300], P('frames'), as said below
- centroids: float32 [384, 3, 300], P('frames'), as said below
- assignment: int32 [5120], P('frames'), may hold values from 0 to 383, as said below
- home_row: int32 [384], replicated, may hold values from 0 to 383, as said below
- pair_index: int32 [2, 45056], P(None, 'pairs'), may hold values from 0 to 299, as said below
- mean_dist: float32 [45056], P('pairs'), may hold values from 2 to 5
- tica_weight: bfloat16 [45056, 100], P('pairs'), may hold values from -0.02734375 to 0.02734375
Outputs:
- tica_proj: float32 [5120, 100], P('frames', 'pairs')
- new_centroids: float32 [384, 3, 300], P('frames')
- occupancy: float32 [384], P('frames')
The draws below stay inside these ranges and needn't reach their ends.
Inputs may be any that keep to these rules, and one draw needn't show every extreme that they name: `assignment`: microstate m is kept by index home_row[m] // 48 of frames. The frames of one device (an aligned block of 640 rows) name microstates of any one such index at most 160 times, and of some index exactly 160 times, in every block. `home_row`: each number appears once. `pair_index`: the two residues of a pair differ. `coords`: positions in nanometres. `centroids`: positions in nanometres.
All inputs are finite; a program needn't handle non-finite values.
Results may differ from the reference program's by a relative error of at most 0.0029.
Values sent between devices are 32-bit elements; how exact they have to be, the bound alone decides.
No kernel may reach another device: no remote copies, remote signals or barrier semaphores. Data moves between devices by JAX's collectives and lax.ppermute only.
A program may use at most 128 MiB of HBM per device.

```python
import math
import jax
import jax.numpy as jnp
from jax import lax

RES = 300
K = 100
F_DEV = 640
MS_DEV = 48
NEWTON = 8
PAIRS = 45056
FRAMES = 5120
M = 384
CAP = 160
N_FRAMES = 8


def route_tables(key):
    base_key = jax.random.fold_in(key, 101)
    subkeys = jax.random.split(base_key, 6)
    home_row = jax.random.permutation(subkeys[0], M).astype(jnp.int32)
    inverse = jnp.argsort(home_row).astype(jnp.int32)
    hottest = jax.random.randint(subkeys[1], (N_FRAMES, 1), 0, N_FRAMES)
    runner = (hottest + jax.random.randint(subkeys[2], (N_FRAMES, 1), 1, N_FRAMES)) % N_FRAMES
    runner_count = jax.random.randint(subkeys[3], (N_FRAMES, 1), 1, CAP + 1)
    frame_order = jax.vmap(lambda subkey: jax.random.permutation(subkey, F_DEV))(jax.random.split(subkeys[4], N_FRAMES)).astype(jnp.int32)
    remaining = jnp.maximum(frame_order - CAP - runner_count, 0) % (N_FRAMES - 2)
    low_owner = jnp.minimum(hottest, runner)
    high_owner = jnp.maximum(hottest, runner)
    remaining = remaining + (remaining >= low_owner).astype(jnp.int32)
    remaining = remaining + (remaining >= high_owner).astype(jnp.int32)
    owner_dev = jnp.where(frame_order < CAP, hottest, jnp.where(frame_order < CAP + runner_count, runner, remaining))
    local_slot = jax.random.randint(subkeys[5], (N_FRAMES, F_DEV), 0, MS_DEV)
    assignment = inverse[(owner_dev * MS_DEV + local_slot).reshape(-1)]
    return (home_row, assignment.astype(jnp.int32))


def base_structures(key):
    base_key = jax.random.fold_in(key, 202)
    spread = jnp.array([2.0, 1.4, 1.0], jnp.float32)
    return jax.random.normal(base_key, (M, 3, RES), jnp.float32) * spread[None, :, None]


def draw_home_row(key, part):
    home_row, assignment = route_tables(key)
    return home_row


def draw_assignment(key, part):
    home_row, assignment = route_tables(key)
    return assignment


def draw_centroids(key, part):
    structure = base_structures(key)
    key = jax.random.fold_in(key, 3)
    noise = 0.15 * jax.random.normal(key, (M, 3, RES), jnp.float32)
    return structure + noise


def draw_coords(key, part):
    home_row, assignment = route_tables(key)
    structure = base_structures(key)
    key = jax.random.fold_in(key, 5)
    subkeys = jax.random.split(key, 4)
    quaternion = jax.random.normal(subkeys[0], (FRAMES, 4), jnp.float32)
    quaternion = quaternion / jnp.sqrt(jnp.sum(quaternion * quaternion, axis=1, keepdims=True))
    qw, qx, qy, qz = (quaternion[:, 0], quaternion[:, 1], quaternion[:, 2], quaternion[:, 3])
    rotation = jnp.stack([jnp.stack([1 - 2 * (qy * qy + qz * qz), 2 * (qx * qy - qw * qz), 2 * (qx * qz + qw * qy)], axis=1), jnp.stack([2 * (qx * qy + qw * qz), 1 - 2 * (qx * qx + qz * qz), 2 * (qy * qz - qw * qx)], axis=1), jnp.stack([2 * (qx * qz - qw * qy), 2 * (qy * qz + qw * qx), 1 - 2 * (qx * qx + qy * qy)], axis=1)], axis=1)
    frame_base = structure[home_row[assignment]]
    rotated = jnp.einsum('fab,fbr->far', rotation, frame_base)
    noise_scale = jnp.exp(jax.random.uniform(subkeys[1], (FRAMES, 1, 1), jnp.float32, jnp.log(0.2), jnp.log(0.6)))
    noise = jax.random.normal(subkeys[2], (FRAMES, 3, RES), jnp.float32)
    shift = 3.0 * jax.random.normal(subkeys[3], (FRAMES, 3, 1), jnp.float32)
    return rotated + noise_scale * noise + shift


def draw_pair_index(key, part):
    key = jax.random.fold_in(key, 9)
    subkeys = jax.random.split(key, 2)
    first_res = jax.random.randint(subkeys[0], (PAIRS,), 0, RES)
    offset = jax.random.randint(subkeys[1], (PAIRS,), 1, RES)
    second_res = (first_res + offset) % RES
    return jnp.stack([first_res, second_res]).astype(jnp.int32)


def steps_of(own_key, extent, cuts, low, largest):
    def one(axis_at, parts):
        steps = jax.random.uniform(jax.random.fold_in(jax.random.fold_in(own_key, 6), axis_at), (parts,), jnp.float32, low / len(cuts), largest / len(cuts))
        return jnp.repeat(jnp.exp(steps), extent[axis_at] // parts).reshape((-1,) + (1,) * (len(extent) - axis_at - 1))

    gain = one(*cuts[0])
    for cut in cuts[1:]:
        gain = gain * one(*cut)
    return gain


def bell_draw(key, shape, scale, reach, cuts=(), kind=jnp.bfloat16):
    factor_of = steps_of(key, shape, cuts, -0.22, 0.18) if cuts else 1.0
    entries = jax.random.normal(key, shape, jnp.float32) * scale * factor_of
    return jnp.minimum(jnp.maximum(entries, -reach), reach).astype(kind)


def setup_inputs(seed: int = 0) -> dict:
    keys = jax.random.split(jax.random.key(seed), 8)
    return {
        "coords": draw_coords(jax.random.fold_in(keys[7], 71), 0),
        "centroids": draw_centroids(jax.random.fold_in(keys[7], 71), 0),
        "assignment": draw_assignment(jax.random.fold_in(keys[7], 71), 0),
        "home_row": draw_home_row(jax.random.fold_in(keys[7], 71), 0),
        "pair_index": draw_pair_index(jax.random.fold_in(keys[7], 71), 0),
        "mean_dist": jnp.clip(2.0 + 3.0 * jax.random.uniform(keys[5], (PAIRS,), jnp.float32) ** steps_of(keys[5], (PAIRS,), ((0, 4),), -0.2, 0.2), 2.0, 5.0),
        "tica_weight": bell_draw(keys[6], (PAIRS, K), PAIRS ** -0.5, 0.02734375, ((0, 4),)),
    }


prior_weight = 4.0

def polar_factor(cross):
    scale = jnp.sqrt(lax.optimization_barrier(jnp.sum(cross * cross, axis=(0, 1))))
    matrix = cross / scale
    for newton_step in range(NEWTON):
        entry = [[matrix[i, j] for j in range(3)] for i in range(3)]
        cofactor = [[entry[(i + 1) % 3][(j + 1) % 3] * entry[(i + 2) % 3][(j + 2) % 3] - entry[(i + 1) % 3][(j + 2) % 3] * entry[(i + 2) % 3][(j + 1) % 3] for j in range(3)] for i in range(3)]
        determinant = entry[0][0] * cofactor[0][0] + entry[0][1] * cofactor[0][1] + entry[0][2] * cofactor[0][2]
        stacked = jnp.stack([jnp.stack(line) for line in cofactor])
        matrix = 0.5 * (matrix + stacked / determinant)
    return matrix

def align_frames(centered, refs):
    cross = jnp.einsum('bar,bcr->acb', refs, centered, precision=lax.Precision.HIGHEST)
    rotation = polar_factor(cross)
    return jnp.einsum('acb,bcr->bar', rotation, centered, precision=lax.Precision.HIGHEST)

def reference(coords, centroids, assignment, home_row, pair_index, mean_dist, tica_weight):
    block_rows = math.gcd(FRAMES, 256)

    def project_block(block):
        first_pos = block[:, :, pair_index[0]]
        second_pos = block[:, :, pair_index[1]]
        diff = first_pos - second_pos
        distance = jnp.sqrt(lax.optimization_barrier(jnp.sum(diff * diff, axis=1)))
        feature = (distance - mean_dist[None, :]).astype(jnp.bfloat16)
        return jnp.dot(feature, tica_weight, preferred_element_type=jnp.float32)
    blocks = coords.reshape(FRAMES // block_rows, block_rows, 3, RES)
    tica_proj = lax.map(project_block, blocks).reshape(FRAMES, K)
    weight = 1.0 / (1.0 + 4.0 * lax.optimization_barrier(jnp.mean(tica_proj * tica_proj, axis=1)))
    frame_row = home_row[assignment].astype(jnp.int32)
    centered = coords - lax.optimization_barrier(jnp.mean(coords, axis=2, keepdims=True))
    ref_centered = centroids - lax.optimization_barrier(jnp.mean(centroids, axis=2, keepdims=True))
    aligned = align_frames(centered, ref_centered[frame_row])
    occupancy = jax.ops.segment_sum(weight, frame_row, num_segments=M)
    summed = jax.ops.segment_sum(weight[:, None, None] * aligned, frame_row, num_segments=M)
    new_centroids = (prior_weight * ref_centered + summed) / (prior_weight + occupancy[:, None, None])
    return (tica_proj, new_centroids, occupancy)
```

```python
import functools

import jax
import jax.numpy as jnp
from jax import lax
from jax.experimental import pallas as pl
from jax.experimental.pallas import tpu as pltpu
from jax.sharding import PartitionSpec as P

NEWTON = 8
PIECES = 3
VMEM_BYTES = 60 * 2**20

prior_weight = 4.0
piece_type = jnp.float8_e4m3fn


def round_up(value, multiple):
    return -(-value // multiple) * multiple


def center_rows(rows):
    return rows - jnp.sum(rows, axis=0, keepdims=True) / rows.shape[0]


def load_pieces(coords_ref, split_ref, positions_ref, unit_ref, stride):
    dims, res_count, frames = coords_ref.shape
    centered = [center_rows(coords_ref[c]) for c in range(dims)]
    reach = functools.reduce(
        jnp.maximum, [jnp.max(jnp.abs(rows), axis=0, keepdims=True) for rows in centered]
    )
    reach = jnp.maximum(reach, 1e-30)
    unit_ref[...] = jnp.broadcast_to(reach * (1.0 / 256.0), (128, frames)).T
    scale = 256.0 / reach
    split_ref[...] = jnp.zeros_like(split_ref)
    for c in range(dims):
        rest = centered[c] * scale
        for k in range(PIECES):
            piece = rest.astype(piece_type).astype(jnp.float32)
            split_ref[k * stride : k * stride + res_count, :] = piece
            rest = rest - piece
        positions_ref[c * frames : (c + 1) * frames, :] = split_ref[...].T.astype(piece_type)


def project_kernel(
    axis, share, index_ref, mean_ref, weight_ref, coords_ref, *refs
):
    out_refs = refs[:-5]
    split_ref, positions_ref, unit_ref, selector_ref, total_ref = refs[-5:]
    dims, res_count, frames = coords_ref.shape
    comps, pairs = weight_ref.shape
    step = pl.program_id(0)
    stride = round_up(res_count, 32)

    @pl.when(step == 0)
    def _():
        load_pieces(coords_ref, split_ref, positions_ref, unit_ref, stride)
        total_ref[...] = jnp.zeros_like(total_ref)
        selector_ref[...] = jnp.zeros_like(selector_ref)

    residue = lax.broadcasted_iota(jnp.int32, (stride, pairs), 0)
    selector = (
        jnp.where(residue == index_ref[0:1, :], 1.0, 0.0)
        - jnp.where(residue == index_ref[1:2, :], 1.0, 0.0)
    ).astype(piece_type)
    for k in range(PIECES):
        selector_ref[k * stride : (k + 1) * stride, :] = selector
    square = None
    for c in range(dims):
        diff = jnp.dot(
            positions_ref[c * frames : (c + 1) * frames, :],
            selector_ref[...],
            preferred_element_type=jnp.float32,
        )
        square = diff * diff if square is None else square + diff * diff
    distance = square * lax.rsqrt(jnp.maximum(square, 1e-37)) * unit_ref[:, 0:1]
    feature = (distance - mean_ref[0:1, :]).astype(jnp.bfloat16)
    total_ref[:, 0:comps] += lax.dot_general(
        feature,
        weight_ref[...],
        (((1,), (1,)), ((), ())),
        preferred_element_type=jnp.float32,
    )

    @pl.when(step == pl.num_programs(0) - 1)
    def _():
        flipped = total_ref[...].T
        parts = len(out_refs)
        rows = [flipped[k * share : (k + 1) * share, :] for k in range(parts)]
        me = lax.axis_index(axis)
        for s, out_ref in enumerate(out_refs):
            owner = lax.rem(me + s, parts)
            value = rows[0]
            for k in range(1, parts):
                value = jnp.where(owner == k, rows[k], value)
            out_ref[...] = value


def project(coords, pair_index, mean_dist, tica_weight, axis):
    dims, res_count, frames = coords.shape
    comps, pairs = tica_weight.shape
    parts = lax.axis_size(axis)
    share = comps // parts
    block = next(b for b in (2816, 1408, 1024, 512, 256, 128, pairs) if pairs % b == 0)
    depth = round_up(PIECES * round_up(res_count, 32), 256)
    return pl.pallas_call(
        functools.partial(project_kernel, axis, share),
        grid=(pairs // block,),
        in_specs=[
            pl.BlockSpec((2, block), lambda i: (0, i)),
            pl.BlockSpec((1, block), lambda i: (0, i)),
            pl.BlockSpec((comps, block), lambda i: (0, i)),
            pl.BlockSpec((dims, res_count, frames), lambda i: (0, 0, 0)),
        ],
        out_specs=[pl.BlockSpec((share, frames), lambda i: (0, 0))] * parts,
        out_shape=[jax.ShapeDtypeStruct((share, frames), jnp.float32)] * parts,
        scratch_shapes=[
            pltpu.VMEM((depth, frames), jnp.float32),
            pltpu.VMEM((dims * frames, depth), piece_type),
            pltpu.VMEM((frames, 128), jnp.float32),
            pltpu.VMEM((depth, block), piece_type),
            pltpu.VMEM((frames, round_up(comps, 128)), jnp.float32),
        ],
        compiler_params=pltpu.CompilerParams(vmem_limit_bytes=VMEM_BYTES),
        cost_estimate=pl.CostEstimate(
            flops=2 * dims * frames * pairs * depth, bytes_accessed=8 * 2**20, transcendentals=0
        ),
        name="project",
    )(pair_index, mean_dist, tica_weight, coords)


def polar_factor(cross):
    size = sum(cross[i][j] * cross[i][j] for i in range(3) for j in range(3))
    size = jnp.sqrt(size)
    entry = [[cross[i][j] / size for j in range(3)] for i in range(3)]
    for newton_step in range(NEWTON):
        cofactor = [
            [
                entry[(i + 1) % 3][(j + 1) % 3] * entry[(i + 2) % 3][(j + 2) % 3]
                - entry[(i + 1) % 3][(j + 2) % 3] * entry[(i + 2) % 3][(j + 1) % 3]
                for j in range(3)
            ]
            for i in range(3)
        ]
        determinant = (
            entry[0][0] * cofactor[0][0]
            + entry[0][1] * cofactor[0][1]
            + entry[0][2] * cofactor[0][2]
        )
        inverse = 1.0 / determinant
        entry = [
            [0.5 * (entry[i][j] + cofactor[i][j] * inverse) for j in range(3)] for i in range(3)
        ]
    return entry


def align_kernel(frames_axis, pairs_axis, quarter, coords_ref, assigned_ref, home_ref, *refs):
    parts = len(refs) - 4
    piece_refs = refs[:parts]
    member_ref, aligned_ref, refs_ref, centered_ref = refs[parts:]
    dims, res_count, frames = coords_ref.shape
    micro = home_ref.shape[1]
    local_micro = piece_refs[0].shape[1]
    me = lax.axis_index(frames_axis)
    for s, piece_ref in enumerate(piece_refs):
        owner = lax.rem(me + parts - s, parts)
        at = pl.multiple_of(owner * local_micro, 8)
        refs_ref[:, pl.ds(at, local_micro), :] = piece_ref[...]

    state = lax.broadcasted_iota(jnp.int32, (micro, frames), 0)
    chosen = (state == assigned_ref[...]).astype(jnp.float32).astype(jnp.bfloat16)
    home = home_ref[...]
    half = lax.broadcasted_iota(jnp.int32, (16, micro), 0)
    halves = jnp.where(half == 0, home >> 5, jnp.where(half == 1, home & 31, 0))
    picked = jnp.dot(
        halves.astype(jnp.float32).astype(jnp.bfloat16), chosen, preferred_element_type=jnp.float32
    )
    frame_row = (picked[0:1, :] * 32.0 + picked[1:2, :]).astype(jnp.int32)
    member = (state == frame_row).astype(jnp.float32).astype(jnp.bfloat16)
    member_ref[...] = member

    centered = [center_rows(coords_ref[c]) for c in range(dims)]
    centered_ref[...] = jnp.zeros_like(centered_ref)
    for c in range(dims):
        centered_ref[c, 0:res_count, :] = centered[c]
    cross = []
    for a in range(dims):
        rows = refs_ref[a]
        rows = (rows - jnp.sum(rows, axis=1, keepdims=True) / res_count).T
        high = rows.astype(jnp.bfloat16)
        low = (rows - high.astype(jnp.float32)).astype(jnp.bfloat16)
        own = jnp.dot(high, member, preferred_element_type=jnp.float32) + jnp.dot(
            low, member, preferred_element_type=jnp.float32
        )
        cross.append([jnp.sum(own * centered[b], axis=0, keepdims=True) for b in range(dims)])
    rotation = polar_factor(cross)
    start = pl.multiple_of(lax.axis_index(pairs_axis) * quarter, 8)
    mine = [centered_ref[b, pl.ds(start, quarter), :] for b in range(dims)]
    for a in range(dims):
        aligned_ref[a * quarter : (a + 1) * quarter, :] = sum(
            rotation[a][b] * mine[b] for b in range(dims)
        )


def align(coords, assignment, home_row, pieces, frames_axis, pairs_axis, quarter):
    dims, res_count, frames = coords.shape
    micro = home_row.shape[1]
    whole = quarter * lax.axis_size(pairs_axis)
    return pl.pallas_call(
        functools.partial(align_kernel, frames_axis, pairs_axis, quarter),
        out_shape=[
            jax.ShapeDtypeStruct((micro, frames), jnp.bfloat16),
            jax.ShapeDtypeStruct((dims * quarter, frames), jnp.float32),
        ],
        scratch_shapes=[
            pltpu.VMEM((dims, micro, res_count), jnp.float32),
            pltpu.VMEM((dims, whole, frames), jnp.float32),
        ],
        compiler_params=pltpu.CompilerParams(vmem_limit_bytes=VMEM_BYTES),
        cost_estimate=pl.CostEstimate(
            flops=8 * dims * frames * micro * res_count, bytes_accessed=2**22, transcendentals=0
        ),
        name="align",
    )(coords, assignment, home_row, *pieces)


def gather_kernel(axis, comps, member_ref, aligned_ref, *refs):
    square_refs = refs[:-3]
    out_ref, square_ref, weighted_ref = refs[-3:]
    parts = len(square_refs)
    me = lax.axis_index(axis)
    for s, ref in enumerate(square_refs):
        square_ref[lax.rem(me + parts - s, parts)] = ref[...]
    square = sum(square_ref[k] for k in range(parts))
    weight = 1.0 / (1.0 + 4.0 * (square / comps))
    rows = aligned_ref.shape[0]
    width, frames = weighted_ref.shape
    weighted_ref[0:rows, :] = aligned_ref[...] * weight
    tail = lax.broadcasted_iota(jnp.int32, (width - rows, frames), 0)
    weighted_ref[rows:, :] = jnp.where(tail == 0, weight, 0.0)
    weighted = weighted_ref[...]
    high = weighted.astype(jnp.bfloat16)
    low = (weighted - high.astype(jnp.float32)).astype(jnp.bfloat16)
    member = member_ref[...]
    over_frames = (((1,), (1,)), ((), ()))
    summed = lax.dot_general(
        member, high, over_frames, preferred_element_type=jnp.float32
    ) + lax.dot_general(member, low, over_frames, preferred_element_type=jnp.float32)
    out_ref[...] = summed.reshape(out_ref.shape)


def gather(member, aligned, squares, axis, comps, owners):
    micro, frames = member.shape
    rows = aligned.shape[0]
    width = round_up(rows + 1, 128)
    return pl.pallas_call(
        functools.partial(gather_kernel, axis, comps),
        out_shape=jax.ShapeDtypeStruct((owners, micro // owners, width), jnp.float32),
        scratch_shapes=[
            pltpu.VMEM((len(squares), 1, frames), jnp.float32),
            pltpu.VMEM((width, frames), jnp.float32),
        ],
        compiler_params=pltpu.CompilerParams(vmem_limit_bytes=VMEM_BYTES),
        name="gather",
    )(member, aligned, *squares)


def update_kernel(axis, quarter, centroids_ref, *refs):
    piece_refs = refs[:-3]
    out_ref, occupancy_ref, pieces_ref = refs[-3:]
    parts = len(piece_refs)
    dims, states, res_count = centroids_ref.shape
    me = lax.axis_index(axis)
    for s, ref in enumerate(piece_refs):
        pieces_ref[lax.rem(me + parts - s, parts)] = ref[...]
    occupancy = pieces_ref[0][:, dims * quarter : dims * quarter + 1]
    row = lax.broadcasted_iota(jnp.int32, (states, states), 0)
    column = lax.broadcasted_iota(jnp.int32, (states, states), 1)
    occupancy_ref[...] = jnp.sum(jnp.where(row == column, occupancy, 0.0), axis=0, keepdims=True)
    divisor = prior_weight + occupancy
    for c in range(dims):
        rows = centroids_ref[c]
        rows = rows - jnp.sum(rows, axis=1, keepdims=True) / res_count
        for z in range(parts):
            low, high = z * quarter, min((z + 1) * quarter, res_count)
            summed = pieces_ref[z][:, c * quarter : c * quarter + high - low]
            out_ref[c, :, low:high] = (prior_weight * rows[:, low:high] + summed) / divisor


def update(centroids, pieces, axis, quarter):
    dims, states, res_count = centroids.shape
    return pl.pallas_call(
        functools.partial(update_kernel, axis, quarter),
        out_shape=[
            jax.ShapeDtypeStruct((dims, states, res_count), jnp.float32),
            jax.ShapeDtypeStruct((1, states), jnp.float32),
        ],
        scratch_shapes=[pltpu.VMEM((len(pieces),) + pieces[0].shape, jnp.float32)],
        compiler_params=pltpu.CompilerParams(vmem_limit_bytes=VMEM_BYTES),
        name="update",
    )(centroids, *pieces)


def from_behind(value, axis, step):
    size = lax.axis_size(axis)
    return lax.ppermute(value, axis, [(i, (i + step) % size) for i in range(size)])


def gathered(value, axis):
    return [value] + [from_behind(value, axis, s) for s in range(1, lax.axis_size(axis))]


def local(coords, centroids, assignment, home_row, pair_index, mean_dist, tica_weight):
    comps = tica_weight.shape[1]
    parts = lax.axis_size("pairs")
    owners = lax.axis_size("frames")
    coords = jnp.transpose(coords, (1, 2, 0))
    centroids = jnp.transpose(centroids, (1, 0, 2))
    quarter = round_up(-(-coords.shape[1] // parts), 8)

    refs = gathered(centroids, "frames")
    partial = project(coords, pair_index, mean_dist[None, :], tica_weight.T, "pairs")
    tica = partial[0]
    for s in range(1, parts):
        tica = tica + from_behind(partial[s], "pairs", s)
    member, aligned = align(
        coords, assignment[None, :], home_row[None, :], refs, "frames", "pairs", quarter
    )
    squares = gathered(jnp.sum(tica * tica, axis=0, keepdims=True), "pairs")
    sums = gather(member, aligned, squares, "pairs", comps, owners)
    sums = lax.all_to_all(sums, "frames", split_axis=0, concat_axis=0, tiled=True)
    sums = jnp.sum(sums, axis=0)
    new_centroids, occupancy = update(centroids, gathered(sums, "pairs"), "pairs", quarter)
    return (tica.T, jnp.transpose(new_centroids, (1, 0, 2)), occupancy[0])


def solution(mesh):
    in_specs = (
        P("frames", None, None),
        P("frames", None, None),
        P("frames"),
        P(),
        P(None, "pairs"),
        P("pairs"),
        P("pairs", None),
    )
    out_specs = (P("frames", "pairs"), P("frames", None, None), P("frames"))
    return jax.shard_map(local, mesh=mesh, in_specs=in_specs, out_specs=out_specs, check_vma=False)
```

```python
import functools

import jax
import jax.numpy as jnp
from jax import lax
from jax.experimental import pallas as pl
from jax.experimental.pallas import tpu as pltpu
from jax.sharding import PartitionSpec as P

NEWTON = 8
PIECES = 3
MIB = 2**20

prior_weight = 4.0
piece_type = jnp.float8_e4m3fn


def round_up(value, multiple):
    return -(-value // multiple) * multiple


def center_rows(rows):
    return rows - jnp.sum(rows, axis=0, keepdims=True) / rows.shape[0]


LANES = 128
DEPTH = 8 * LANES
HALF = LANES // 2
REACH = 247.0


def tail_lanes(res_count):
    tail = res_count - 2 * LANES
    assert 0 < tail <= HALF
    return tail


def split_kernel(coords_ref, positions_ref, unit_ref, rows_ref):
    dims, res_count, frames = coords_ref.shape
    tail = tail_lanes(res_count)
    centered = [center_rows(coords_ref[c]) for c in range(dims)]
    reach = functools.reduce(
        jnp.maximum, [jnp.max(jnp.abs(rows), axis=0, keepdims=True) for rows in centered]
    )
    reach = jnp.maximum(reach, 1e-30)
    unit_ref[...] = jnp.broadcast_to(reach * (1.0 / REACH), (128, frames)).T
    scale = REACH / reach
    rows_ref[res_count:, :] = jnp.zeros((rows_ref.shape[0] - res_count, frames), jnp.float32)
    lane = lax.broadcasted_iota(jnp.int32, (frames, LANES), 1)
    for c in range(dims):
        rows_ref[0:res_count, :] = centered[c] * scale
        rest = rows_ref[...].T
        pieces = []
        for k in range(PIECES - 1):
            shift = 1.5 * 2.0**23 * 16.0 / 32.0**k
            pieces.append((rest + shift) - shift)
            rest = rest - pieces[-1]
        pieces.append(rest)
        high, mid, low = [
            [piece[:, g * LANES : (g + 1) * LANES] for g in range(3)] for piece in pieces
        ]
        mixed = jnp.where(lane < tail, high[2], mid[1])
        shared = jnp.concatenate([mid[1][:, 0:HALF], mid[2][:, 0:HALF]], axis=1)
        groups = [high[0], high[1], mixed, mid[0], low[0], low[1], low[2], shared]
        for g, group in enumerate(groups):
            positions_ref[c * frames : (c + 1) * frames, g * LANES : (g + 1) * LANES] = group.astype(
                piece_type
            )


def split_coords(coords):
    dims, res_count, frames = coords.shape
    return pl.pallas_call(
        split_kernel,
        out_shape=[
            jax.ShapeDtypeStruct((dims * frames, DEPTH), piece_type),
            jax.ShapeDtypeStruct((frames, 128), jnp.float32),
        ],
        scratch_shapes=[pltpu.VMEM((round_up(res_count, 128), frames), jnp.float32)],
        compiler_params=pltpu.CompilerParams(vmem_limit_bytes=24 * MIB),
        cost_estimate=pl.CostEstimate(
            flops=2**30, bytes_accessed=2**23, transcendentals=0
        ),
        name="split",
    )(coords)


def project_kernel(
    axis, share, res_count, index_ref, mean_ref, weight_ref, positions_ref, unit_ref, *refs
):
    out_refs = refs[:-2]
    selector_ref, total_ref = refs[-2:]
    comps, pairs = weight_ref.shape
    frames = unit_ref.shape[0]
    dims = positions_ref.shape[0] // frames
    tail = tail_lanes(res_count)
    step = pl.program_id(0)

    @pl.when(step == 0)
    def _():
        total_ref[...] = jnp.zeros_like(total_ref)

    def select(residue):
        return (
            jnp.where(residue == index_ref[0:1, :], 1.0, 0.0)
            - jnp.where(residue == index_ref[1:2, :], 1.0, 0.0)
        ).astype(piece_type)

    line = lax.broadcasted_iota(jnp.int32, (LANES, pairs), 0)
    firsts, lasts = select(line), select(line + 2 * LANES)
    middle = select(line + LANES)
    shared = select(
        jnp.where(line < HALF, jnp.where(line < tail, line + LANES, -1), line + 2 * LANES - HALF)
    )
    mixed = select(jnp.where(line < tail, line + 2 * LANES, line + LANES))
    groups = [firsts, middle, mixed, firsts, firsts, middle, lasts, shared]
    for g, group in enumerate(groups):
        selector_ref[g * LANES : (g + 1) * LANES, :] = group
    square = None
    for c in range(dims):
        diff = jnp.dot(
            positions_ref[c * frames : (c + 1) * frames, :],
            selector_ref[...],
            preferred_element_type=jnp.float32,
        )
        square = diff * diff if square is None else square + diff * diff
    distance = square * lax.rsqrt(jnp.maximum(square, 1e-37)) * unit_ref[:, 0:1]
    feature = (distance - mean_ref[0:1, :]).astype(jnp.bfloat16)
    total_ref[:, 0:comps] += lax.dot_general(
        feature,
        weight_ref[...],
        (((1,), (1,)), ((), ())),
        preferred_element_type=jnp.float32,
    )

    @pl.when(step == pl.num_programs(0) - 1)
    def _():
        flipped = total_ref[...].T
        parts = len(out_refs)
        rows = [flipped[k * share : (k + 1) * share, :] for k in range(parts)]
        me = lax.axis_index(axis)
        for s, out_ref in enumerate(out_refs):
            value = rows[0]
            for k in range(1, parts):
                value = jnp.where(me ^ s == k, rows[k], value)
            out_ref[...] = value


def project(positions, unit, res_count, pair_index, mean_dist, tica_weight, axis):
    frames = unit.shape[0]
    comps, pairs = tica_weight.shape
    parts = lax.axis_size(axis)
    share = comps // parts
    block = next(b for b in (2816, 1408, 1024, 512, 256, 128, pairs) if pairs % b == 0)
    depth = positions.shape[1]
    return pl.pallas_call(
        functools.partial(project_kernel, axis, share, res_count),
        grid=(pairs // block,),
        in_specs=[
            pl.BlockSpec((2, block), lambda i: (0, i)),
            pl.BlockSpec((1, block), lambda i: (0, i)),
            pl.BlockSpec((comps, block), lambda i: (0, i)),
            pl.BlockSpec(positions.shape, lambda i: (0, 0)),
            pl.BlockSpec(unit.shape, lambda i: (0, 0)),
        ],
        out_specs=[pl.BlockSpec((share, frames), lambda i: (0, 0))] * parts,
        out_shape=[jax.ShapeDtypeStruct((share, frames), jnp.float32)] * parts,
        scratch_shapes=[
            pltpu.VMEM((depth, block), piece_type),
            pltpu.VMEM((frames, round_up(comps, 128)), jnp.float32),
        ],
        compiler_params=pltpu.CompilerParams(vmem_limit_bytes=48 * MIB),
        cost_estimate=pl.CostEstimate(
            flops=2 * positions.shape[0] * pairs * depth,
            bytes_accessed=8 * 2**20,
            transcendentals=0,
        ),
        name="project",
    )(pair_index, mean_dist, tica_weight, positions, unit)


def polar_factor(cross):
    size = sum(cross[i][j] * cross[i][j] for i in range(3) for j in range(3))
    size = jnp.sqrt(size)
    entry = [[cross[i][j] / size for j in range(3)] for i in range(3)]
    for newton_step in range(NEWTON):
        cofactor = [
            [
                entry[(i + 1) % 3][(j + 1) % 3] * entry[(i + 2) % 3][(j + 2) % 3]
                - entry[(i + 1) % 3][(j + 2) % 3] * entry[(i + 2) % 3][(j + 1) % 3]
                for j in range(3)
            ]
            for i in range(3)
        ]
        determinant = (
            entry[0][0] * cofactor[0][0]
            + entry[0][1] * cofactor[0][1]
            + entry[0][2] * cofactor[0][2]
        )
        inverse = 1.0 / determinant
        entry = [
            [0.5 * (entry[i][j] + cofactor[i][j] * inverse) for j in range(3)] for i in range(3)
        ]
    return entry


def align_kernel(frames_axis, pairs_axis, quarter, coords_ref, assigned_ref, home_ref, *refs):
    parts = len(refs) - 4
    piece_refs = refs[:parts]
    member_ref, aligned_ref, refs_ref, centered_ref = refs[parts:]
    dims, res_count, frames = coords_ref.shape
    micro = home_ref.shape[0]
    both, local_micro = piece_refs[0].shape[0], piece_refs[0].shape[2]
    me = lax.axis_index(frames_axis)
    for s, piece_ref in enumerate(piece_refs):
        for k in range(both):
            owner = me ^ (both * s + k)
            at = pl.multiple_of(owner * local_micro, 8)
            refs_ref[:, pl.ds(at, local_micro), :] = piece_ref[k]

    state = lax.broadcasted_iota(jnp.int32, (micro, frames), 0)
    chosen = (state == assigned_ref[...].reshape(1, frames)).astype(jnp.float32).astype(jnp.bfloat16)
    home = home_ref[...].reshape(1, micro)
    half = lax.broadcasted_iota(jnp.int32, (16, micro), 0)
    halves = jnp.where(half == 0, home >> 5, jnp.where(half == 1, home & 31, 0))
    picked = jnp.dot(
        halves.astype(jnp.float32).astype(jnp.bfloat16), chosen, preferred_element_type=jnp.float32
    )
    frame_row = (picked[0:1, :] * 32.0 + picked[1:2, :]).astype(jnp.int32)
    member = (state == frame_row).astype(jnp.float32).astype(jnp.bfloat16)
    member_ref[...] = member

    centered = [center_rows(coords_ref[c]) for c in range(dims)]
    centered_ref[...] = jnp.zeros_like(centered_ref)
    for c in range(dims):
        centered_ref[c, 0:res_count, :] = centered[c]
    cross = []
    for a in range(dims):
        rows = refs_ref[a]
        rows = (rows - jnp.sum(rows, axis=1, keepdims=True) / res_count).T
        high = rows.astype(jnp.bfloat16)
        low = (rows - high.astype(jnp.float32)).astype(jnp.bfloat16)
        own = jnp.dot(high, member, preferred_element_type=jnp.float32) + jnp.dot(
            low, member, preferred_element_type=jnp.float32
        )
        cross.append([jnp.sum(own * centered[b], axis=0, keepdims=True) for b in range(dims)])
    rotation = polar_factor(cross)
    start = pl.multiple_of(lax.axis_index(pairs_axis) * quarter, 8)
    mine = [centered_ref[b, pl.ds(start, quarter), :] for b in range(dims)]
    for a in range(dims):
        aligned_ref[a * quarter : (a + 1) * quarter, :] = sum(
            rotation[a][b] * mine[b] for b in range(dims)
        )


def align(coords, assignment, home_row, pieces, frames_axis, pairs_axis, quarter):
    dims, res_count, frames = coords.shape
    micro = home_row.shape[0]
    whole = quarter * lax.axis_size(pairs_axis)
    return pl.pallas_call(
        functools.partial(align_kernel, frames_axis, pairs_axis, quarter),
        out_shape=[
            jax.ShapeDtypeStruct((micro, frames), jnp.bfloat16),
            jax.ShapeDtypeStruct((dims * quarter, frames), jnp.float32),
        ],
        scratch_shapes=[
            pltpu.VMEM((dims, micro, res_count), jnp.float32),
            pltpu.VMEM((dims, whole, frames), jnp.float32),
        ],
        compiler_params=pltpu.CompilerParams(vmem_limit_bytes=40 * MIB),
        cost_estimate=pl.CostEstimate(
            flops=8 * dims * frames * micro * res_count, bytes_accessed=2**22, transcendentals=0
        ),
        name="align",
    )(coords, assignment, home_row, *pieces)


def gather_kernel(axis, owners_axis, comps, parts, member_ref, aligned_ref, *refs):
    square_refs = refs[:parts]
    out_refs, (square_ref, weighted_ref, summed_ref) = refs[parts:-3], refs[-3:]
    me = lax.axis_index(axis)
    for s, ref in enumerate(square_refs):
        square_ref[me ^ s] = ref[...]
    square = sum(square_ref[k] for k in range(parts))
    weight = 1.0 / (1.0 + 4.0 * (square / comps))
    rows = aligned_ref.shape[0]
    width, frames = weighted_ref.shape
    weighted_ref[0:rows, :] = aligned_ref[...] * weight
    tail = lax.broadcasted_iota(jnp.int32, (width - rows, frames), 0)
    weighted_ref[rows:, :] = jnp.where(tail == 0, weight, 0.0)
    weighted = weighted_ref[...]
    high = weighted.astype(jnp.bfloat16)
    low = (weighted - high.astype(jnp.float32)).astype(jnp.bfloat16)
    member = member_ref[...]
    over_frames = (((1,), (1,)), ((), ()))
    summed_ref[...] = lax.dot_general(
        member, high, over_frames, preferred_element_type=jnp.float32
    ) + lax.dot_general(member, low, over_frames, preferred_element_type=jnp.float32)
    here = lax.axis_index(owners_axis)
    for k, out_ref in enumerate(out_refs):
        states = out_ref.shape[1]
        for s in range(out_ref.shape[0]):
            at = pl.multiple_of((here ^ (2 * s + k)) * states, 8)
            out_ref[s] = summed_ref[pl.ds(at, states), :]


def gather(member, aligned, squares, axis, owners_axis, comps):
    micro, frames = member.shape
    owners = lax.axis_size(owners_axis)
    rows = aligned.shape[0]
    width = round_up(rows + 1, 128)
    return pl.pallas_call(
        functools.partial(gather_kernel, axis, owners_axis, comps, len(squares)),
        out_shape=[jax.ShapeDtypeStruct((owners // 2, micro // owners, width), jnp.float32)] * 2,
        scratch_shapes=[
            pltpu.VMEM((len(squares), 1, frames), jnp.float32),
            pltpu.VMEM((width, frames), jnp.float32),
            pltpu.VMEM((micro, width), jnp.float32),
        ],
        compiler_params=pltpu.CompilerParams(vmem_limit_bytes=16 * MIB),
        name="gather",
    )(member, aligned, *squares)


def merge_kernel(mine_ref, other_ref, *out_refs):
    for s, out_ref in enumerate(out_refs):
        out_ref[...] = mine_ref[s] + other_ref[s]


def merge(mine, other):
    count = mine.shape[0]
    return pl.pallas_call(
        merge_kernel,
        out_shape=[jax.ShapeDtypeStruct(mine.shape[1:], jnp.float32)] * count,
        compiler_params=pltpu.CompilerParams(vmem_limit_bytes=8 * MIB),
        name="merge",
    )(mine, other)


def update_kernel(axis, quarter, centroids_ref, *refs):
    piece_refs = refs[:-3]
    out_ref, occupancy_ref, pieces_ref = refs[-3:]
    parts = len(piece_refs)
    dims, states, res_count = centroids_ref.shape
    me = lax.axis_index(axis)
    for s, ref in enumerate(piece_refs):
        pieces_ref[me ^ s] = ref[...]
    occupancy = pieces_ref[0][:, dims * quarter : dims * quarter + 1]
    row = lax.broadcasted_iota(jnp.int32, (states, states), 0)
    column = lax.broadcasted_iota(jnp.int32, (states, states), 1)
    occupancy_ref[...] = jnp.sum(jnp.where(row == column, occupancy, 0.0), axis=0, keepdims=True)
    divisor = prior_weight + occupancy
    for c in range(dims):
        rows = centroids_ref[c]
        rows = rows - jnp.sum(rows, axis=1, keepdims=True) / res_count
        for z in range(parts):
            low, high = z * quarter, min((z + 1) * quarter, res_count)
            summed = pieces_ref[z][:, c * quarter : c * quarter + high - low]
            out_ref[c, :, low:high] = (prior_weight * rows[:, low:high] + summed) / divisor


def update(centroids, pieces, axis, quarter):
    dims, states, res_count = centroids.shape
    return pl.pallas_call(
        functools.partial(update_kernel, axis, quarter),
        out_shape=[
            jax.ShapeDtypeStruct((dims, states, res_count), jnp.float32),
            jax.ShapeDtypeStruct((1, states), jnp.float32),
        ],
        scratch_shapes=[pltpu.VMEM((len(pieces),) + pieces[0].shape, jnp.float32)],
        compiler_params=pltpu.CompilerParams(vmem_limit_bytes=8 * MIB),
        name="update",
    )(centroids, *pieces)


def swap(value, axis, step):
    size = lax.axis_size(axis)
    return lax.ppermute(value, axis, [(i, i ^ step) for i in range(size)])


def gathered(value, axis, first=1):
    steps = range(first, lax.axis_size(axis), first)
    return [value] + [swap(value, axis, s) for s in steps]


def local(coords, centroids, assignment, home_row, pair_index, mean_dist, tica_weight):
    comps = tica_weight.shape[1]
    parts = lax.axis_size("pairs")
    coords = jnp.transpose(coords, (1, 2, 0))
    centroids = jnp.transpose(centroids, (1, 0, 2))
    quarter = round_up(-(-coords.shape[1] // parts), 8)

    other = swap(centroids, "frames", 1)
    positions, unit = split_coords(coords)
    positions, both = lax.optimization_barrier((positions, jnp.stack([centroids, other])))
    refs = gathered(both, "frames", 2)
    partial = project(
        positions, unit, coords.shape[1], pair_index, mean_dist[None, :], tica_weight.T, "pairs"
    )
    partial, refs = lax.optimization_barrier((partial, refs))
    received = [swap(partial[s], "pairs", s) for s in range(1, parts)]
    member, aligned, received = lax.optimization_barrier(
        (
            *align(coords, assignment, home_row, refs, "frames", "pairs", quarter),
            received,
        )
    )
    tica = partial[0]
    for piece in received:
        tica = tica + piece
    squares = gathered(jnp.sum(tica * tica, axis=0, keepdims=True), "pairs")
    mine, other = gather(member, aligned, squares, "pairs", "frames", comps)
    sums = merge(mine, swap(other, "frames", 1))
    total = sums[0]
    for s in range(1, len(sums)):
        total = total + swap(sums[s], "frames", 2 * s)
    new_centroids, occupancy = update(centroids, gathered(total, "pairs"), "pairs", quarter)
    return (tica.T, jnp.transpose(new_centroids, (1, 0, 2)), occupancy[0])


def solution(mesh):
    in_specs = (
        P("frames", None, None),
        P("frames", None, None),
        P("frames"),
        P(),
        P(None, "pairs"),
        P("pairs"),
        P("pairs", None),
    )
    out_specs = (P("frames", "pairs"), P("frames", None, None), P("frames"))
    return jax.shard_map(local, mesh=mesh, in_specs=in_specs, out_specs=out_specs, check_vma=False)
```

```python
import functools

import jax
import jax.numpy as jnp
from jax import lax
from jax.experimental import pallas as pl
from jax.experimental.pallas import tpu as pltpu
from jax.sharding import PartitionSpec as P

NEWTON = 8
PIECES = 3
MIB = 2**20

prior_weight = 4.0
piece_type = jnp.float8_e4m3fn


def round_up(value, multiple):
    return -(-value // multiple) * multiple


def center_rows(rows):
    return rows - jnp.sum(rows, axis=0, keepdims=True) / rows.shape[0]


LANES = 128
DEPTH = 8 * LANES
HALF = LANES // 2
REACH = 247.0


def tail_lanes(res_count):
    tail = res_count - 2 * LANES
    assert 0 < tail <= HALF
    return tail


def split_kernel(coords_ref, positions_ref, unit_ref, rows_ref):
    dims, res_count, frames = coords_ref.shape
    tail = tail_lanes(res_count)
    centered = [center_rows(coords_ref[c]) for c in range(dims)]
    reach = functools.reduce(
        jnp.maximum, [jnp.max(jnp.abs(rows), axis=0, keepdims=True) for rows in centered]
    )
    reach = jnp.maximum(reach, 1e-30)
    unit_ref[...] = jnp.broadcast_to(reach * (1.0 / REACH), (128, frames)).T
    scale = REACH / reach
    rows_ref[res_count:, :] = jnp.zeros((rows_ref.shape[0] - res_count, frames), jnp.float32)
    lane = lax.broadcasted_iota(jnp.int32, (frames, LANES), 1)
    for c in range(dims):
        rows_ref[0:res_count, :] = centered[c] * scale
        rest = rows_ref[...].T
        pieces = []
        for k in range(PIECES - 1):
            shift = 1.5 * 2.0**23 * 16.0 / 32.0**k
            pieces.append((rest + shift) - shift)
            rest = rest - pieces[-1]
        pieces.append(rest)
        high, mid, low = [
            [piece[:, g * LANES : (g + 1) * LANES] for g in range(3)] for piece in pieces
        ]
        mixed = jnp.where(lane < tail, high[2], mid[1])
        shared = jnp.concatenate([mid[1][:, 0:HALF], mid[2][:, 0:HALF]], axis=1)
        groups = [high[0], high[1], mixed, mid[0], low[0], low[1], low[2], shared]
        for g, group in enumerate(groups):
            positions_ref[c * frames : (c + 1) * frames, g * LANES : (g + 1) * LANES] = group.astype(
                piece_type
            )


def split_coords(coords):
    dims, res_count, frames = coords.shape
    return pl.pallas_call(
        split_kernel,
        out_shape=[
            jax.ShapeDtypeStruct((dims * frames, DEPTH), piece_type),
            jax.ShapeDtypeStruct((frames, 128), jnp.float32),
        ],
        scratch_shapes=[pltpu.VMEM((round_up(res_count, 128), frames), jnp.float32)],
        compiler_params=pltpu.CompilerParams(vmem_limit_bytes=24 * MIB),
        cost_estimate=pl.CostEstimate(
            flops=2**30, bytes_accessed=2**23, transcendentals=0
        ),
        name="split",
    )(coords)


def project_kernel(
    axis, share, res_count, index_ref, mean_ref, weight_ref, positions_ref, unit_ref, *refs
):
    out_refs = refs[:-2]
    selector_ref, total_ref = refs[-2:]
    comps, pairs = weight_ref.shape
    frames = unit_ref.shape[0]
    dims = positions_ref.shape[0] // frames
    tail = tail_lanes(res_count)
    step = pl.program_id(0)

    @pl.when(step == 0)
    def _():
        total_ref[...] = jnp.zeros_like(total_ref)

    def select(residue):
        return (
            jnp.where(residue == index_ref[0:1, :], 1.0, 0.0)
            - jnp.where(residue == index_ref[1:2, :], 1.0, 0.0)
        ).astype(piece_type)

    line = lax.broadcasted_iota(jnp.int32, (LANES, pairs), 0)
    firsts, lasts = select(line), select(line + 2 * LANES)
    middle = select(line + LANES)
    shared = select(
        jnp.where(line < HALF, jnp.where(line < tail, line + LANES, -1), line + 2 * LANES - HALF)
    )
    mixed = select(jnp.where(line < tail, line + 2 * LANES, line + LANES))
    groups = [firsts, middle, mixed, firsts, firsts, middle, lasts, shared]
    for g, group in enumerate(groups):
        selector_ref[g * LANES : (g + 1) * LANES, :] = group
    square = None
    for c in range(dims):
        diff = jnp.dot(
            positions_ref[c * frames : (c + 1) * frames, :],
            selector_ref[...],
            preferred_element_type=jnp.float32,
        )
        square = diff * diff if square is None else square + diff * diff
    distance = square * lax.rsqrt(jnp.maximum(square, 1e-37)) * unit_ref[:, 0:1]
    feature = (distance - mean_ref[0:1, :]).astype(jnp.bfloat16)
    total_ref[:, 0:comps] += lax.dot_general(
        feature,
        weight_ref[...],
        (((1,), (1,)), ((), ())),
        preferred_element_type=jnp.float32,
    )

    @pl.when(step == pl.num_programs(0) - 1)
    def _():
        flipped = total_ref[...].T
        parts = len(out_refs)
        rows = [flipped[k * share : (k + 1) * share, :] for k in range(parts)]
        me = lax.axis_index(axis)
        for s, out_ref in enumerate(out_refs):
            value = rows[0]
            for k in range(1, parts):
                value = jnp.where(me ^ s == k, rows[k], value)
            for j in range(frames // LANES):
                out_ref[j * share : (j + 1) * share, :] = value[:, j * LANES : (j + 1) * LANES]


def project(positions, unit, res_count, pair_index, mean_dist, tica_weight, axis):
    frames = unit.shape[0]
    comps, pairs = tica_weight.shape
    parts = lax.axis_size(axis)
    share = comps // parts
    block = next(b for b in (2816, 1408, 1024, 512, 256, 128, pairs) if pairs % b == 0)
    depth = positions.shape[1]
    return pl.pallas_call(
        functools.partial(project_kernel, axis, share, res_count),
        grid=(pairs // block,),
        in_specs=[
            pl.BlockSpec((2, block), lambda i: (0, i)),
            pl.BlockSpec((1, block), lambda i: (0, i)),
            pl.BlockSpec((comps, block), lambda i: (0, i)),
            pl.BlockSpec(positions.shape, lambda i: (0, 0)),
            pl.BlockSpec(unit.shape, lambda i: (0, 0)),
        ],
        out_specs=[pl.BlockSpec((share * frames // LANES, LANES), lambda i: (0, 0))] * parts,
        out_shape=[jax.ShapeDtypeStruct((share * frames // LANES, LANES), jnp.float32)] * parts,
        scratch_shapes=[
            pltpu.VMEM((depth, block), piece_type),
            pltpu.VMEM((frames, round_up(comps, 128)), jnp.float32),
        ],
        compiler_params=pltpu.CompilerParams(vmem_limit_bytes=48 * MIB),
        cost_estimate=pl.CostEstimate(
            flops=2 * positions.shape[0] * pairs * depth,
            bytes_accessed=8 * 2**20,
            transcendentals=0,
        ),
        name="project",
    )(pair_index, mean_dist, tica_weight, positions, unit)


def finish_kernel(*refs):
    part_refs, (tica_ref, square_ref) = refs[:-2], refs[-2:]
    share, frames = tica_ref.shape
    total = sum(ref[...] for ref in part_refs)
    for j in range(frames // LANES):
        part = total[j * share : (j + 1) * share, :]
        tica_ref[:, j * LANES : (j + 1) * LANES] = part
        square_ref[:, j * LANES : (j + 1) * LANES] = jnp.sum(part * part, axis=0, keepdims=True)


def finish(partial, frames):
    share = partial[0].size // frames
    return pl.pallas_call(
        finish_kernel,
        out_shape=[
            jax.ShapeDtypeStruct((share, frames), jnp.float32),
            jax.ShapeDtypeStruct((1, frames), jnp.float32),
        ],
        compiler_params=pltpu.CompilerParams(vmem_limit_bytes=8 * MIB),
        name="finish",
    )(*partial)


def polar_factor(cross):
    size = sum(cross[i][j] * cross[i][j] for i in range(3) for j in range(3))
    size = jnp.sqrt(size)
    entry = [[cross[i][j] / size for j in range(3)] for i in range(3)]
    for newton_step in range(NEWTON):
        cofactor = [
            [
                entry[(i + 1) % 3][(j + 1) % 3] * entry[(i + 2) % 3][(j + 2) % 3]
                - entry[(i + 1) % 3][(j + 2) % 3] * entry[(i + 2) % 3][(j + 1) % 3]
                for j in range(3)
            ]
            for i in range(3)
        ]
        determinant = (
            entry[0][0] * cofactor[0][0]
            + entry[0][1] * cofactor[0][1]
            + entry[0][2] * cofactor[0][2]
        )
        inverse = 1.0 / determinant
        entry = [
            [0.5 * (entry[i][j] + cofactor[i][j] * inverse) for j in range(3)] for i in range(3)
        ]
    return entry


def align_kernel(frames_axis, pairs_axis, quarter, coords_ref, assigned_ref, home_ref, *refs):
    parts = len(refs) - 4
    piece_refs = refs[:parts]
    member_ref, aligned_ref, refs_ref, centered_ref = refs[parts:]
    dims, res_count, frames = coords_ref.shape
    micro = home_ref.shape[0]
    both, local_micro = piece_refs[0].shape[0], piece_refs[0].shape[2]
    me = lax.axis_index(frames_axis)
    for s, piece_ref in enumerate(piece_refs):
        for k in range(both):
            owner = me ^ (both * s + k)
            at = pl.multiple_of(owner * local_micro, 8)
            refs_ref[:, pl.ds(at, local_micro), :] = piece_ref[k]

    state = lax.broadcasted_iota(jnp.int32, (micro, frames), 0)
    chosen = (state == assigned_ref[...].reshape(1, frames)).astype(jnp.float32).astype(jnp.bfloat16)
    home = home_ref[...].reshape(1, micro)
    half = lax.broadcasted_iota(jnp.int32, (16, micro), 0)
    halves = jnp.where(half == 0, home >> 5, jnp.where(half == 1, home & 31, 0))
    picked = jnp.dot(
        halves.astype(jnp.float32).astype(jnp.bfloat16), chosen, preferred_element_type=jnp.float32
    )
    frame_row = (picked[0:1, :] * 32.0 + picked[1:2, :]).astype(jnp.int32)
    member = (state == frame_row).astype(jnp.float32).astype(jnp.bfloat16)
    member_ref[...] = member

    centered = [center_rows(coords_ref[c]) for c in range(dims)]
    centered_ref[...] = jnp.zeros_like(centered_ref)
    for c in range(dims):
        centered_ref[c, 0:res_count, :] = centered[c]
    cross = []
    for a in range(dims):
        rows = refs_ref[a]
        rows = (rows - jnp.sum(rows, axis=1, keepdims=True) / res_count).T
        high = rows.astype(jnp.bfloat16)
        low = (rows - high.astype(jnp.float32)).astype(jnp.bfloat16)
        own = jnp.dot(high, member, preferred_element_type=jnp.float32) + jnp.dot(
            low, member, preferred_element_type=jnp.float32
        )
        cross.append([jnp.sum(own * centered[b], axis=0, keepdims=True) for b in range(dims)])
    rotation = polar_factor(cross)
    start = pl.multiple_of(lax.axis_index(pairs_axis) * quarter, 8)
    mine = [centered_ref[b, pl.ds(start, quarter), :] for b in range(dims)]
    for a in range(dims):
        aligned_ref[a * quarter : (a + 1) * quarter, :] = sum(
            rotation[a][b] * mine[b] for b in range(dims)
        )


def align(coords, assignment, home_row, pieces, frames_axis, pairs_axis, quarter):
    dims, res_count, frames = coords.shape
    micro = home_row.shape[0]
    whole = quarter * lax.axis_size(pairs_axis)
    return pl.pallas_call(
        functools.partial(align_kernel, frames_axis, pairs_axis, quarter),
        out_shape=[
            jax.ShapeDtypeStruct((micro, frames), jnp.bfloat16),
            jax.ShapeDtypeStruct((dims * quarter, frames), jnp.float32),
        ],
        scratch_shapes=[
            pltpu.VMEM((dims, micro, res_count), jnp.float32),
            pltpu.VMEM((dims, whole, frames), jnp.float32),
        ],
        compiler_params=pltpu.CompilerParams(vmem_limit_bytes=40 * MIB),
        cost_estimate=pl.CostEstimate(
            flops=8 * dims * frames * micro * res_count, bytes_accessed=2**22, transcendentals=0
        ),
        name="align",
    )(coords, assignment, home_row, *pieces)


def gather_kernel(axis, owners_axis, comps, parts, member_ref, aligned_ref, *refs):
    square_refs = refs[:parts]
    out_refs, (square_ref, weighted_ref, summed_ref) = refs[parts:-3], refs[-3:]
    me = lax.axis_index(axis)
    for s, ref in enumerate(square_refs):
        square_ref[me ^ s] = ref[...]
    square = sum(square_ref[k] for k in range(parts))
    weight = 1.0 / (1.0 + 4.0 * (square / comps))
    rows = aligned_ref.shape[0]
    width, frames = weighted_ref.shape
    weighted_ref[0:rows, :] = aligned_ref[...] * weight
    tail = lax.broadcasted_iota(jnp.int32, (width - rows, frames), 0)
    weighted_ref[rows:, :] = jnp.where(tail == 0, weight, 0.0)
    weighted = weighted_ref[...]
    high = weighted.astype(jnp.bfloat16)
    low = (weighted - high.astype(jnp.float32)).astype(jnp.bfloat16)
    member = member_ref[...]
    over_frames = (((1,), (1,)), ((), ()))
    summed_ref[...] = lax.dot_general(
        member, high, over_frames, preferred_element_type=jnp.float32
    ) + lax.dot_general(member, low, over_frames, preferred_element_type=jnp.float32)
    here = lax.axis_index(owners_axis)
    for k, out_ref in enumerate(out_refs):
        states = out_ref.shape[1]
        for s in range(out_ref.shape[0]):
            at = pl.multiple_of((here ^ (2 * s + k)) * states, 8)
            out_ref[s] = summed_ref[pl.ds(at, states), :]


def gather(member, aligned, squares, axis, owners_axis, comps):
    micro, frames = member.shape
    owners = lax.axis_size(owners_axis)
    rows = aligned.shape[0]
    width = round_up(rows + 1, 128)
    return pl.pallas_call(
        functools.partial(gather_kernel, axis, owners_axis, comps, len(squares)),
        out_shape=[jax.ShapeDtypeStruct((owners // 2, micro // owners, width), jnp.float32)] * 2,
        scratch_shapes=[
            pltpu.VMEM((len(squares), 1, frames), jnp.float32),
            pltpu.VMEM((width, frames), jnp.float32),
            pltpu.VMEM((micro, width), jnp.float32),
        ],
        compiler_params=pltpu.CompilerParams(vmem_limit_bytes=16 * MIB),
        name="gather",
    )(member, aligned, *squares)


def merge_kernel(mine_ref, other_ref, *out_refs):
    for s, out_ref in enumerate(out_refs):
        out_ref[...] = mine_ref[s] + other_ref[s]


def merge(mine, other):
    count = mine.shape[0]
    return pl.pallas_call(
        merge_kernel,
        out_shape=[jax.ShapeDtypeStruct(mine.shape[1:], jnp.float32)] * count,
        compiler_params=pltpu.CompilerParams(vmem_limit_bytes=8 * MIB),
        name="merge",
    )(mine, other)


def update_kernel(axis, quarter, centroids_ref, *refs):
    piece_refs = refs[:-3]
    out_ref, occupancy_ref, pieces_ref = refs[-3:]
    parts = len(piece_refs)
    dims, states, res_count = centroids_ref.shape
    me = lax.axis_index(axis)
    for s, ref in enumerate(piece_refs):
        pieces_ref[me ^ s] = ref[...]
    occupancy = pieces_ref[0][:, dims * quarter : dims * quarter + 1]
    row = lax.broadcasted_iota(jnp.int32, (states, states), 0)
    column = lax.broadcasted_iota(jnp.int32, (states, states), 1)
    occupancy_ref[...] = jnp.sum(jnp.where(row == column, occupancy, 0.0), axis=0, keepdims=True)
    divisor = prior_weight + occupancy
    for c in range(dims):
        rows = centroids_ref[c]
        rows = rows - jnp.sum(rows, axis=1, keepdims=True) / res_count
        for z in range(parts):
            low, high = z * quarter, min((z + 1) * quarter, res_count)
            summed = pieces_ref[z][:, c * quarter : c * quarter + high - low]
            out_ref[c, :, low:high] = (prior_weight * rows[:, low:high] + summed) / divisor


def update(centroids, pieces, axis, quarter):
    dims, states, res_count = centroids.shape
    return pl.pallas_call(
        functools.partial(update_kernel, axis, quarter),
        out_shape=[
            jax.ShapeDtypeStruct((dims, states, res_count), jnp.float32),
            jax.ShapeDtypeStruct((1, states), jnp.float32),
        ],
        scratch_shapes=[pltpu.VMEM((len(pieces),) + pieces[0].shape, jnp.float32)],
        compiler_params=pltpu.CompilerParams(vmem_limit_bytes=8 * MIB),
        name="update",
    )(centroids, *pieces)


def swap(value, axis, step):
    size = lax.axis_size(axis)
    return lax.ppermute(value, axis, [(i, i ^ step) for i in range(size)])


def gathered(value, axis, first=1):
    steps = range(first, lax.axis_size(axis), first)
    return [value] + [swap(value, axis, s) for s in steps]


def local(coords, centroids, assignment, home_row, pair_index, mean_dist, tica_weight):
    comps = tica_weight.shape[1]
    parts = lax.axis_size("pairs")
    coords = jnp.transpose(coords, (1, 2, 0))
    centroids = jnp.transpose(centroids, (1, 0, 2))
    quarter = round_up(-(-coords.shape[1] // parts), 8)

    other = swap(centroids, "frames", 1)
    positions, unit = split_coords(coords)
    positions, both = lax.optimization_barrier((positions, jnp.stack([centroids, other])))
    refs = gathered(both, "frames", 2)
    partial = project(
        positions, unit, coords.shape[1], pair_index, mean_dist[None, :], tica_weight.T, "pairs"
    )
    partial, refs = lax.optimization_barrier((partial, refs))
    received = [swap(partial[s], "pairs", s) for s in reversed(range(1, parts))]
    member, aligned, received = lax.optimization_barrier(
        (
            *align(coords, assignment, home_row, refs, "frames", "pairs", quarter),
            received,
        )
    )
    tica, square = finish([partial[0], *received], coords.shape[2])
    squares = gathered(square, "pairs")
    mine, other = gather(member, aligned, squares, "pairs", "frames", comps)
    sums = merge(mine, swap(other, "frames", 1))
    total = sums[0]
    for s in range(1, len(sums)):
        total = total + swap(sums[s], "frames", 2 * s)
    new_centroids, occupancy = update(centroids, gathered(total, "pairs"), "pairs", quarter)
    return (tica.T, jnp.transpose(new_centroids, (1, 0, 2)), occupancy[0])


def solution(mesh):
    in_specs = (
        P("frames", None, None),
        P("frames", None, None),
        P("frames"),
        P(),
        P(None, "pairs"),
        P("pairs"),
        P("pairs", None),
    )
    out_specs = (P("frames", "pairs"), P("frames", None, None), P("frames"))
    return jax.shard_map(local, mesh=mesh, in_specs=in_specs, out_specs=out_specs, check_vma=False)
```

```python
import functools

import jax
import jax.numpy as jnp
from jax import lax
from jax.experimental import pallas as pl
from jax.experimental.pallas import tpu as pltpu
from jax.sharding import PartitionSpec as P

NEWTON = 8
PIECES = 3
MIB = 2**20

prior_weight = 4.0
piece_type = jnp.float8_e4m3fn


def round_up(value, multiple):
    return -(-value // multiple) * multiple


def center_rows(rows):
    return rows - jnp.sum(rows, axis=0, keepdims=True) / rows.shape[0]


LANES = 128
DEPTH = 8 * LANES
HALF = LANES // 2
REACH = 247.0


def tail_lanes(res_count):
    tail = res_count - 2 * LANES
    assert 0 < tail <= HALF
    return tail


def split_kernel(coords_ref, positions_ref, unit_ref, rows_ref):
    dims, res_count, frames = coords_ref.shape
    tail = tail_lanes(res_count)
    centered = [center_rows(coords_ref[c]) for c in range(dims)]
    reach = functools.reduce(
        jnp.maximum, [jnp.max(jnp.abs(rows), axis=0, keepdims=True) for rows in centered]
    )
    reach = jnp.maximum(reach, 1e-30)
    unit_ref[...] = jnp.broadcast_to(reach * (1.0 / REACH), (128, frames)).T
    scale = REACH / reach
    rows_ref[res_count:, :] = jnp.zeros((rows_ref.shape[0] - res_count, frames), jnp.float32)
    lane = lax.broadcasted_iota(jnp.int32, (frames, LANES), 1)
    for c in range(dims):
        rows_ref[0:res_count, :] = centered[c] * scale
        rest = rows_ref[...].T
        pieces = []
        for k in range(PIECES - 1):
            shift = 1.5 * 2.0**23 * 16.0 / 32.0**k
            pieces.append((rest + shift) - shift)
            rest = rest - pieces[-1]
        pieces.append(rest)
        high, mid, low = [
            [piece[:, g * LANES : (g + 1) * LANES] for g in range(3)] for piece in pieces
        ]
        mixed = jnp.where(lane < tail, high[2], mid[1])
        shared = jnp.concatenate([mid[1][:, 0:HALF], mid[2][:, 0:HALF]], axis=1)
        groups = [high[0], high[1], mixed, mid[0], low[0], low[1], low[2], shared]
        for g, group in enumerate(groups):
            positions_ref[c * frames : (c + 1) * frames, g * LANES : (g + 1) * LANES] = group.astype(
                piece_type
            )


def split_coords(coords):
    dims, res_count, frames = coords.shape
    return pl.pallas_call(
        split_kernel,
        out_shape=[
            jax.ShapeDtypeStruct((dims * frames, DEPTH), piece_type),
            jax.ShapeDtypeStruct((frames, 128), jnp.float32),
        ],
        scratch_shapes=[pltpu.VMEM((round_up(res_count, 128), frames), jnp.float32)],
        compiler_params=pltpu.CompilerParams(vmem_limit_bytes=24 * MIB),
        cost_estimate=pl.CostEstimate(
            flops=2**30, bytes_accessed=2**23, transcendentals=0
        ),
        name="split",
    )(coords)


def project_kernel(
    axis, share, res_count, index_ref, mean_ref, weight_ref, positions_ref, unit_ref, *refs
):
    out_refs = refs[:-2]
    selector_ref, total_ref = refs[-2:]
    comps, pairs = weight_ref.shape
    frames = unit_ref.shape[0]
    dims = positions_ref.shape[0] // frames
    tail = tail_lanes(res_count)
    step = pl.program_id(0)

    @pl.when(step == 0)
    def _():
        total_ref[...] = jnp.zeros_like(total_ref)

    def select(residue):
        return (
            jnp.where(residue == index_ref[0:1, :], 1.0, 0.0)
            - jnp.where(residue == index_ref[1:2, :], 1.0, 0.0)
        ).astype(piece_type)

    line = lax.broadcasted_iota(jnp.int32, (LANES, pairs), 0)
    firsts, lasts = select(line), select(line + 2 * LANES)
    middle = select(line + LANES)
    shared = select(
        jnp.where(line < HALF, jnp.where(line < tail, line + LANES, -1), line + 2 * LANES - HALF)
    )
    mixed = select(jnp.where(line < tail, line + 2 * LANES, line + LANES))
    groups = [firsts, middle, mixed, firsts, firsts, middle, lasts, shared]
    for g, group in enumerate(groups):
        selector_ref[g * LANES : (g + 1) * LANES, :] = group
    square = None
    for c in range(dims):
        diff = jnp.dot(
            positions_ref[c * frames : (c + 1) * frames, :],
            selector_ref[...],
            preferred_element_type=jnp.float32,
        )
        square = diff * diff if square is None else square + diff * diff
    distance = square * lax.rsqrt(jnp.maximum(square, 1e-37)) * unit_ref[:, 0:1]
    feature = (distance - mean_ref[0:1, :]).astype(jnp.bfloat16)
    total_ref[:, 0:comps] += lax.dot_general(
        feature,
        weight_ref[...],
        (((1,), (1,)), ((), ())),
        preferred_element_type=jnp.float32,
    )

    @pl.when(step == pl.num_programs(0) - 1)
    def _():
        flipped = total_ref[...].T
        parts = len(out_refs)
        rows = [flipped[k * share : (k + 1) * share, :] for k in range(parts)]
        me = lax.axis_index(axis)
        for s, out_ref in enumerate(out_refs):
            value = rows[0]
            for k in range(1, parts):
                value = jnp.where(me ^ s == k, rows[k], value)
            for j in range(frames // LANES):
                out_ref[j * share : (j + 1) * share, :] = value[:, j * LANES : (j + 1) * LANES]


def project(positions, unit, res_count, pair_index, mean_dist, tica_weight, axis):
    frames = unit.shape[0]
    comps, pairs = tica_weight.shape
    parts = lax.axis_size(axis)
    share = comps // parts
    block = next(b for b in (2816, 1408, 1024, 512, 256, 128, pairs) if pairs % b == 0)
    depth = positions.shape[1]
    return pl.pallas_call(
        functools.partial(project_kernel, axis, share, res_count),
        grid=(pairs // block,),
        in_specs=[
            pl.BlockSpec((2, block), lambda i: (0, i)),
            pl.BlockSpec((1, block), lambda i: (0, i)),
            pl.BlockSpec((comps, block), lambda i: (0, i)),
            pl.BlockSpec(positions.shape, lambda i: (0, 0)),
            pl.BlockSpec(unit.shape, lambda i: (0, 0)),
        ],
        out_specs=[pl.BlockSpec((share * frames // LANES, LANES), lambda i: (0, 0))] * parts,
        out_shape=[jax.ShapeDtypeStruct((share * frames // LANES, LANES), jnp.float32)] * parts,
        scratch_shapes=[
            pltpu.VMEM((depth, block), piece_type),
            pltpu.VMEM((frames, round_up(comps, 128)), jnp.float32),
        ],
        compiler_params=pltpu.CompilerParams(vmem_limit_bytes=48 * MIB),
        cost_estimate=pl.CostEstimate(
            flops=2 * positions.shape[0] * pairs * depth,
            bytes_accessed=8 * 2**20,
            transcendentals=0,
        ),
        name="project",
    )(pair_index, mean_dist, tica_weight, positions, unit)


def finish_kernel(*refs):
    part_refs, (tica_ref, square_ref) = refs[:-2], refs[-2:]
    share, frames = tica_ref.shape
    total = sum(ref[...] for ref in part_refs)
    for j in range(frames // LANES):
        part = total[j * share : (j + 1) * share, :]
        tica_ref[:, j * LANES : (j + 1) * LANES] = part
        square_ref[:, j * LANES : (j + 1) * LANES] = jnp.sum(part * part, axis=0, keepdims=True)


def finish(partial, frames):
    share = partial[0].size // frames
    return pl.pallas_call(
        finish_kernel,
        out_shape=[
            jax.ShapeDtypeStruct((share, frames), jnp.float32),
            jax.ShapeDtypeStruct((1, frames), jnp.float32),
        ],
        compiler_params=pltpu.CompilerParams(vmem_limit_bytes=8 * MIB),
        name="finish",
    )(*partial)


def polar_factor(cross):
    size = sum(cross[i][j] * cross[i][j] for i in range(3) for j in range(3))
    size = jnp.sqrt(size)
    entry = [[cross[i][j] / size for j in range(3)] for i in range(3)]
    for newton_step in range(NEWTON):
        cofactor = [
            [
                entry[(i + 1) % 3][(j + 1) % 3] * entry[(i + 2) % 3][(j + 2) % 3]
                - entry[(i + 1) % 3][(j + 2) % 3] * entry[(i + 2) % 3][(j + 1) % 3]
                for j in range(3)
            ]
            for i in range(3)
        ]
        determinant = (
            entry[0][0] * cofactor[0][0]
            + entry[0][1] * cofactor[0][1]
            + entry[0][2] * cofactor[0][2]
        )
        inverse = 1.0 / determinant
        entry = [
            [0.5 * (entry[i][j] + cofactor[i][j] * inverse) for j in range(3)] for i in range(3)
        ]
    return entry


def align_kernel(frames_axis, pairs_axis, quarter, coords_ref, assigned_ref, home_ref, *refs):
    parts = len(refs) - 4
    piece_refs = refs[:parts]
    member_ref, aligned_ref, refs_ref, centered_ref = refs[parts:]
    dims, res_count, frames = coords_ref.shape
    micro = home_ref.shape[0]
    both, local_micro = piece_refs[0].shape[0], piece_refs[0].shape[2]
    me = lax.axis_index(frames_axis)
    for s, piece_ref in enumerate(piece_refs):
        for k in range(both):
            owner = me ^ (both * s + k)
            at = pl.multiple_of(owner * local_micro, 8)
            refs_ref[:, pl.ds(at, local_micro), :] = piece_ref[k]

    state = lax.broadcasted_iota(jnp.int32, (micro, frames), 0)
    chosen = (state == assigned_ref[...].reshape(1, frames)).astype(jnp.float32).astype(jnp.bfloat16)
    home = home_ref[...].reshape(1, micro)
    half = lax.broadcasted_iota(jnp.int32, (16, micro), 0)
    halves = jnp.where(half == 0, home >> 5, jnp.where(half == 1, home & 31, 0))
    picked = jnp.dot(
        halves.astype(jnp.float32).astype(jnp.bfloat16), chosen, preferred_element_type=jnp.float32
    )
    frame_row = (picked[0:1, :] * 32.0 + picked[1:2, :]).astype(jnp.int32)
    member = (state == frame_row).astype(jnp.float32).astype(jnp.bfloat16)
    member_ref[...] = member

    centered = [center_rows(coords_ref[c]) for c in range(dims)]
    centered_ref[...] = jnp.zeros_like(centered_ref)
    for c in range(dims):
        centered_ref[c, 0:res_count, :] = centered[c]
    cross = []
    for a in range(dims):
        rows = refs_ref[a]
        rows = (rows - jnp.sum(rows, axis=1, keepdims=True) / res_count).T
        high = rows.astype(jnp.bfloat16)
        low = (rows - high.astype(jnp.float32)).astype(jnp.bfloat16)
        own = jnp.dot(high, member, preferred_element_type=jnp.float32) + jnp.dot(
            low, member, preferred_element_type=jnp.float32
        )
        cross.append([jnp.sum(own * centered[b], axis=0, keepdims=True) for b in range(dims)])
    rotation = polar_factor(cross)
    start = pl.multiple_of(lax.axis_index(pairs_axis) * quarter, 8)
    mine = [centered_ref[b, pl.ds(start, quarter), :] for b in range(dims)]
    for a in range(dims):
        aligned_ref[a * quarter : (a + 1) * quarter, :] = sum(
            rotation[a][b] * mine[b] for b in range(dims)
        )


def align(coords, assignment, home_row, pieces, frames_axis, pairs_axis, quarter):
    dims, res_count, frames = coords.shape
    micro = home_row.shape[0]
    whole = quarter * lax.axis_size(pairs_axis)
    return pl.pallas_call(
        functools.partial(align_kernel, frames_axis, pairs_axis, quarter),
        out_shape=[
            jax.ShapeDtypeStruct((micro, frames), jnp.bfloat16),
            jax.ShapeDtypeStruct((dims * quarter, frames), jnp.float32),
        ],
        scratch_shapes=[
            pltpu.VMEM((dims, micro, res_count), jnp.float32),
            pltpu.VMEM((dims, whole, frames), jnp.float32),
        ],
        compiler_params=pltpu.CompilerParams(vmem_limit_bytes=40 * MIB),
        cost_estimate=pl.CostEstimate(
            flops=8 * dims * frames * micro * res_count, bytes_accessed=2**22, transcendentals=0
        ),
        name="align",
    )(coords, assignment, home_row, *pieces)


def gather_kernel(axis, owners_axis, comps, parts, member_ref, aligned_ref, *refs):
    square_refs = refs[:parts]
    out_refs, (square_ref, weighted_ref, summed_ref) = refs[parts:-3], refs[-3:]
    me = lax.axis_index(axis)
    for s, ref in enumerate(square_refs):
        square_ref[me ^ s] = ref[...]
    square = sum(square_ref[k] for k in range(parts))
    weight = 1.0 / (1.0 + 4.0 * (square / comps))
    rows = aligned_ref.shape[0]
    width, frames = weighted_ref.shape
    weighted_ref[0:rows, :] = aligned_ref[...] * weight
    tail = lax.broadcasted_iota(jnp.int32, (width - rows, frames), 0)
    weighted_ref[rows:, :] = jnp.where(tail == 0, weight, 0.0)
    weighted = weighted_ref[...]
    high = weighted.astype(jnp.bfloat16)
    low = (weighted - high.astype(jnp.float32)).astype(jnp.bfloat16)
    member = member_ref[...]
    over_frames = (((1,), (1,)), ((), ()))
    summed_ref[...] = lax.dot_general(
        member, high, over_frames, preferred_element_type=jnp.float32
    ) + lax.dot_general(member, low, over_frames, preferred_element_type=jnp.float32)
    here = lax.axis_index(owners_axis)
    for k, out_ref in enumerate(out_refs):
        states = out_ref.shape[1]
        for s in range(out_ref.shape[0]):
            at = pl.multiple_of((here ^ (2 * s + k)) * states, 8)
            out_ref[s] = summed_ref[pl.ds(at, states), :]


def gather(member, aligned, squares, axis, owners_axis, comps):
    micro, frames = member.shape
    owners = lax.axis_size(owners_axis)
    rows = aligned.shape[0]
    width = round_up(rows + 1, 128)
    return pl.pallas_call(
        functools.partial(gather_kernel, axis, owners_axis, comps, len(squares)),
        out_shape=[jax.ShapeDtypeStruct((owners // 2, micro // owners, width), jnp.float32)] * 2,
        scratch_shapes=[
            pltpu.VMEM((len(squares), 1, frames), jnp.float32),
            pltpu.VMEM((width, frames), jnp.float32),
            pltpu.VMEM((micro, width), jnp.float32),
        ],
        compiler_params=pltpu.CompilerParams(vmem_limit_bytes=16 * MIB),
        name="gather",
    )(member, aligned, *squares)


def merge_kernel(mine_ref, other_ref, *out_refs):
    for s, out_ref in enumerate(out_refs):
        out_ref[...] = mine_ref[s] + other_ref[s]


def merge(mine, other):
    count = mine.shape[0]
    return pl.pallas_call(
        merge_kernel,
        out_shape=[jax.ShapeDtypeStruct(mine.shape[1:], jnp.float32)] * count,
        compiler_params=pltpu.CompilerParams(vmem_limit_bytes=8 * MIB),
        name="merge",
    )(mine, other)


def update_kernel(axis, quarter, centroids_ref, *refs):
    piece_refs = refs[:-3]
    out_ref, occupancy_ref, pieces_ref = refs[-3:]
    parts = len(piece_refs)
    dims, states, res_count = centroids_ref.shape
    me = lax.axis_index(axis)
    for s, ref in enumerate(piece_refs):
        pieces_ref[me ^ s] = ref[...]
    occupancy = pieces_ref[0][:, dims * quarter : dims * quarter + 1]
    row = lax.broadcasted_iota(jnp.int32, (states, states), 0)
    column = lax.broadcasted_iota(jnp.int32, (states, states), 1)
    occupancy_ref[...] = jnp.sum(jnp.where(row == column, occupancy, 0.0), axis=0, keepdims=True)
    divisor = prior_weight + occupancy
    for c in range(dims):
        rows = centroids_ref[c]
        rows = rows - jnp.sum(rows, axis=1, keepdims=True) / res_count
        for z in range(parts):
            low, high = z * quarter, min((z + 1) * quarter, res_count)
            summed = pieces_ref[z][:, c * quarter : c * quarter + high - low]
            out_ref[c, :, low:high] = (prior_weight * rows[:, low:high] + summed) / divisor


def update(centroids, pieces, axis, quarter):
    dims, states, res_count = centroids.shape
    return pl.pallas_call(
        functools.partial(update_kernel, axis, quarter),
        out_shape=[
            jax.ShapeDtypeStruct((dims, states, res_count), jnp.float32),
            jax.ShapeDtypeStruct((1, states), jnp.float32),
        ],
        scratch_shapes=[pltpu.VMEM((len(pieces),) + pieces[0].shape, jnp.float32)],
        compiler_params=pltpu.CompilerParams(vmem_limit_bytes=8 * MIB),
        name="update",
    )(centroids, *pieces)


def swap(value, axis, step):
    size = lax.axis_size(axis)
    return lax.ppermute(value, axis, [(i, i ^ step) for i in range(size)])


def gathered(value, axis, first=1):
    steps = range(first, lax.axis_size(axis), first)
    return [value] + [swap(value, axis, s) for s in steps]


def local(coords, centroids, assignment, home_row, pair_index, mean_dist, tica_weight):
    comps = tica_weight.shape[1]
    parts = lax.axis_size("pairs")
    coords = jnp.transpose(coords, (1, 2, 0))
    centroids = jnp.transpose(centroids, (1, 0, 2))
    quarter = round_up(-(-coords.shape[1] // parts), 8)

    other = swap(centroids, "frames", 1)
    positions, unit = split_coords(coords)
    positions, both = lax.optimization_barrier((positions, jnp.stack([centroids, other])))
    refs = gathered(both, "frames", 2)
    partial = project(
        positions, unit, coords.shape[1], pair_index, mean_dist[None, :], tica_weight.T, "pairs"
    )
    partial, refs = lax.optimization_barrier((partial, refs))
    received = [swap(partial[s], "pairs", s) for s in reversed(range(1, parts))]
    member, aligned, received = lax.optimization_barrier(
        (
            *align(coords, assignment, home_row, refs, "frames", "pairs", quarter),
            received,
        )
    )
    tica, square = finish([partial[0], *received], coords.shape[2])
    squares = gathered(square, "pairs")
    mine, other = gather(member, aligned, squares, "pairs", "frames", comps)
    sums = merge(mine, swap(other, "frames", 1))
    total = sums[0]
    for s in reversed(range(1, len(sums))):
        total = total + swap(sums[s], "frames", 2 * s)
    new_centroids, occupancy = update(centroids, gathered(total, "pairs"), "pairs", quarter)
    return (tica.T, jnp.transpose(new_centroids, (1, 0, 2)), occupancy[0])


def solution(mesh):
    in_specs = (
        P("frames", None, None),
        P("frames", None, None),
        P("frames"),
        P(),
        P(None, "pairs"),
        P("pairs"),
        P("pairs", None),
    )
    out_specs = (P("frames", "pairs"), P("frames", None, None), P("frames"))
    return jax.shard_map(local, mesh=mesh, in_specs=in_specs, out_specs=out_specs, check_vma=False)
```

```python
import functools

import jax
import jax.numpy as jnp
from jax import lax
from jax.experimental import pallas as pl
from jax.experimental.pallas import tpu as pltpu
from jax.sharding import PartitionSpec as P

NEWTON = 8
PIECES = 3
MIB = 2**20

prior_weight = 4.0
piece_type = jnp.float8_e4m3fn


def round_up(value, multiple):
    return -(-value // multiple) * multiple


def center_rows(rows):
    return rows - jnp.sum(rows, axis=0, keepdims=True) / rows.shape[0]


LANES = 128
DEPTH = 8 * LANES
HALF = LANES // 2
REACH = 247.0


def tail_lanes(res_count):
    tail = res_count - 2 * LANES
    assert 0 < tail <= HALF
    return tail


def split_kernel(coords_ref, positions_ref, unit_ref, rows_ref):
    dims, res_count, frames = coords_ref.shape
    tail = tail_lanes(res_count)
    centered = [center_rows(coords_ref[c]) for c in range(dims)]
    reach = functools.reduce(
        jnp.maximum, [jnp.max(jnp.abs(rows), axis=0, keepdims=True) for rows in centered]
    )
    reach = jnp.maximum(reach, 1e-30)
    unit_ref[...] = jnp.broadcast_to(reach * (1.0 / REACH), (128, frames)).T
    scale = REACH / reach
    below = res_count // 8 * 8
    rows_ref[below:, :] = jnp.zeros((rows_ref.shape[0] - below, frames), jnp.float32)
    lane = lax.broadcasted_iota(jnp.int32, (frames, LANES), 1)
    for c in range(dims):
        rows_ref[0:res_count, :] = centered[c] * scale
        rest = rows_ref[...].T
        pieces = []
        for k in range(PIECES - 1):
            shift = 1.5 * 2.0**23 * 16.0 / 32.0**k
            pieces.append((rest + shift) - shift)
            rest = rest - pieces[-1]
        pieces.append(rest)
        high, mid, low = [
            [piece[:, g * LANES : (g + 1) * LANES] for g in range(3)] for piece in pieces
        ]
        mixed = jnp.where(lane < tail, high[2], mid[1])
        shared = jnp.concatenate([mid[1][:, 0:HALF], mid[2][:, 0:HALF]], axis=1)
        groups = [high[0], high[1], mixed, mid[0], low[0], low[1], low[2], shared]
        for g, group in enumerate(groups):
            positions_ref[c * frames : (c + 1) * frames, g * LANES : (g + 1) * LANES] = group.astype(
                piece_type
            )


def split_coords(coords):
    dims, res_count, frames = coords.shape
    return pl.pallas_call(
        split_kernel,
        out_shape=[
            jax.ShapeDtypeStruct((dims * frames, DEPTH), piece_type),
            jax.ShapeDtypeStruct((frames, 128), jnp.float32),
        ],
        scratch_shapes=[pltpu.VMEM((round_up(res_count, 128), frames), jnp.float32)],
        compiler_params=pltpu.CompilerParams(vmem_limit_bytes=24 * MIB),
        cost_estimate=pl.CostEstimate(
            flops=2**30, bytes_accessed=2**23, transcendentals=0
        ),
        name="split",
    )(coords)


def project_kernel(
    axis, share, res_count, index_ref, mean_ref, weight_ref, positions_ref, unit_ref, *refs
):
    out_refs = refs[:-2]
    selector_ref, total_ref = refs[-2:]
    comps, pairs = weight_ref.shape
    frames = unit_ref.shape[0]
    dims = positions_ref.shape[0] // frames
    tail = tail_lanes(res_count)
    step = pl.program_id(0)

    @pl.when(step == 0)
    def _():
        total_ref[...] = jnp.zeros_like(total_ref)

    def select(residue):
        return (
            jnp.where(residue == index_ref[0:1, :], 1.0, 0.0)
            - jnp.where(residue == index_ref[1:2, :], 1.0, 0.0)
        ).astype(piece_type)

    line = lax.broadcasted_iota(jnp.int32, (LANES, pairs), 0)
    firsts, lasts = select(line), select(line + 2 * LANES)
    middle = select(line + LANES)
    shared = select(
        jnp.where(line < HALF, jnp.where(line < tail, line + LANES, -1), line + 2 * LANES - HALF)
    )
    mixed = select(jnp.where(line < tail, line + 2 * LANES, line + LANES))
    groups = [firsts, middle, mixed, firsts, firsts, middle, lasts, shared]
    for g, group in enumerate(groups):
        selector_ref[g * LANES : (g + 1) * LANES, :] = group
    square = None
    for c in range(dims):
        diff = jnp.dot(
            positions_ref[c * frames : (c + 1) * frames, :],
            selector_ref[...],
            preferred_element_type=jnp.float32,
        )
        square = diff * diff if square is None else square + diff * diff
    distance = square * lax.rsqrt(jnp.maximum(square, 1e-37)) * unit_ref[:, 0:1]
    feature = (distance - mean_ref[0:1, :]).astype(jnp.bfloat16)
    total_ref[:, 0:comps] += lax.dot_general(
        feature,
        weight_ref[...],
        (((1,), (1,)), ((), ())),
        preferred_element_type=jnp.float32,
    )

    @pl.when(step == pl.num_programs(0) - 1)
    def _():
        flipped = total_ref[...].T
        parts = len(out_refs)
        rows = [flipped[k * share : (k + 1) * share, :] for k in range(parts)]
        me = lax.axis_index(axis)
        for s, out_ref in enumerate(out_refs):
            value = rows[0]
            for k in range(1, parts):
                value = jnp.where(me ^ s == k, rows[k], value)
            packed = [value[:, j * LANES : (j + 1) * LANES] for j in range(frames // LANES)]
            spare = out_ref.shape[0] - len(packed) * share
            if spare:
                packed.append(jnp.zeros((spare, LANES), jnp.float32))
            out_ref[...] = jnp.concatenate(packed, axis=0)


def project(positions, unit, res_count, pair_index, mean_dist, tica_weight, axis):
    frames = unit.shape[0]
    comps, pairs = tica_weight.shape
    parts = lax.axis_size(axis)
    share = comps // parts
    packed = round_up(share * frames // LANES, 8)
    block = next(b for b in (2816, 1408, 1024, 512, 256, 128, pairs) if pairs % b == 0)
    depth = positions.shape[1]
    return pl.pallas_call(
        functools.partial(project_kernel, axis, share, res_count),
        grid=(pairs // block,),
        in_specs=[
            pl.BlockSpec((2, block), lambda i: (0, i)),
            pl.BlockSpec((1, block), lambda i: (0, i)),
            pl.BlockSpec((comps, block), lambda i: (0, i)),
            pl.BlockSpec(positions.shape, lambda i: (0, 0)),
            pl.BlockSpec(unit.shape, lambda i: (0, 0)),
        ],
        out_specs=[pl.BlockSpec((packed, LANES), lambda i: (0, 0))] * parts,
        out_shape=[jax.ShapeDtypeStruct((packed, LANES), jnp.float32)] * parts,
        scratch_shapes=[
            pltpu.VMEM((depth, block), piece_type),
            pltpu.VMEM((frames, round_up(comps, 128)), jnp.float32),
        ],
        compiler_params=pltpu.CompilerParams(vmem_limit_bytes=48 * MIB),
        cost_estimate=pl.CostEstimate(
            flops=2 * positions.shape[0] * pairs * depth,
            bytes_accessed=8 * 2**20,
            transcendentals=0,
        ),
        name="project",
    )(pair_index, mean_dist, tica_weight, positions, unit)


def finish_kernel(*refs):
    part_refs, (tica_ref, square_ref) = refs[:-2], refs[-2:]
    share, frames = tica_ref.shape
    total = sum(ref[...] for ref in part_refs)
    for j in range(frames // LANES):
        part = total[j * share : (j + 1) * share, :]
        tica_ref[:, j * LANES : (j + 1) * LANES] = part
        square_ref[:, j * LANES : (j + 1) * LANES] = jnp.sum(part * part, axis=0, keepdims=True)


def finish(partial, share, frames):
    return pl.pallas_call(
        finish_kernel,
        out_shape=[
            jax.ShapeDtypeStruct((share, frames), jnp.float32),
            jax.ShapeDtypeStruct((1, frames), jnp.float32),
        ],
        compiler_params=pltpu.CompilerParams(vmem_limit_bytes=8 * MIB),
        name="finish",
    )(*partial)


def polar_factor(cross):
    size = sum(cross[i][j] * cross[i][j] for i in range(3) for j in range(3))
    size = jnp.sqrt(size)
    entry = [[cross[i][j] / size for j in range(3)] for i in range(3)]
    for newton_step in range(NEWTON):
        cofactor = [
            [
                entry[(i + 1) % 3][(j + 1) % 3] * entry[(i + 2) % 3][(j + 2) % 3]
                - entry[(i + 1) % 3][(j + 2) % 3] * entry[(i + 2) % 3][(j + 1) % 3]
                for j in range(3)
            ]
            for i in range(3)
        ]
        determinant = (
            entry[0][0] * cofactor[0][0]
            + entry[0][1] * cofactor[0][1]
            + entry[0][2] * cofactor[0][2]
        )
        inverse = 1.0 / determinant
        entry = [
            [0.5 * (entry[i][j] + cofactor[i][j] * inverse) for j in range(3)] for i in range(3)
        ]
    return entry


def align_kernel(frames_axis, pairs_axis, quarter, coords_ref, assigned_ref, home_ref, *refs):
    parts = len(refs) - 4
    piece_refs = refs[:parts]
    member_ref, aligned_ref, refs_ref, centered_ref = refs[parts:]
    dims, res_count, frames = coords_ref.shape
    micro = home_ref.shape[0]
    both, local_micro = piece_refs[0].shape[0], piece_refs[0].shape[2]
    me = lax.axis_index(frames_axis)
    for s, piece_ref in enumerate(piece_refs):
        for k in range(both):
            owner = me ^ (both * s + k)
            at = pl.multiple_of(owner * local_micro, 8)
            refs_ref[:, pl.ds(at, local_micro), :] = piece_ref[k]

    state = lax.broadcasted_iota(jnp.int32, (micro, frames), 0)
    chosen = (state == assigned_ref[...].reshape(1, frames)).astype(jnp.float32).astype(jnp.bfloat16)
    home = home_ref[...].reshape(1, micro)
    half = lax.broadcasted_iota(jnp.int32, (16, micro), 0)
    halves = jnp.where(half == 0, home >> 5, jnp.where(half == 1, home & 31, 0))
    picked = jnp.dot(
        halves.astype(jnp.float32).astype(jnp.bfloat16), chosen, preferred_element_type=jnp.float32
    )
    frame_row = (picked[0:1, :] * 32.0 + picked[1:2, :]).astype(jnp.int32)
    member = (state == frame_row).astype(jnp.float32).astype(jnp.bfloat16)
    member_ref[...] = member

    centered = [center_rows(coords_ref[c]) for c in range(dims)]
    centered_ref[...] = jnp.zeros_like(centered_ref)
    for c in range(dims):
        centered_ref[c, 0:res_count, :] = centered[c]
    cross = []
    for a in range(dims):
        rows = refs_ref[a]
        rows = (rows - jnp.sum(rows, axis=1, keepdims=True) / res_count).T
        high = rows.astype(jnp.bfloat16)
        low = (rows - high.astype(jnp.float32)).astype(jnp.bfloat16)
        own = jnp.dot(high, member, preferred_element_type=jnp.float32) + jnp.dot(
            low, member, preferred_element_type=jnp.float32
        )
        cross.append([jnp.sum(own * centered[b], axis=0, keepdims=True) for b in range(dims)])
    rotation = polar_factor(cross)
    start = pl.multiple_of(lax.axis_index(pairs_axis) * quarter, 8)
    mine = [centered_ref[b, pl.ds(start, quarter), :] for b in range(dims)]
    for a in range(dims):
        aligned_ref[a * quarter : (a + 1) * quarter, :] = sum(
            rotation[a][b] * mine[b] for b in range(dims)
        )


def align(coords, assignment, home_row, pieces, frames_axis, pairs_axis, quarter):
    dims, res_count, frames = coords.shape
    micro = home_row.shape[0]
    whole = quarter * lax.axis_size(pairs_axis)
    return pl.pallas_call(
        functools.partial(align_kernel, frames_axis, pairs_axis, quarter),
        out_shape=[
            jax.ShapeDtypeStruct((micro, frames), jnp.bfloat16),
            jax.ShapeDtypeStruct((dims * quarter, frames), jnp.float32),
        ],
        scratch_shapes=[
            pltpu.VMEM((dims, micro, res_count), jnp.float32),
            pltpu.VMEM((dims, whole, frames), jnp.float32),
        ],
        compiler_params=pltpu.CompilerParams(vmem_limit_bytes=40 * MIB),
        cost_estimate=pl.CostEstimate(
            flops=8 * dims * frames * micro * res_count, bytes_accessed=2**22, transcendentals=0
        ),
        name="align",
    )(coords, assignment, home_row, *pieces)


def gather_kernel(axis, owners_axis, comps, parts, member_ref, aligned_ref, *refs):
    square_refs = refs[:parts]
    out_refs, (square_ref, weighted_ref, summed_ref) = refs[parts:-3], refs[-3:]
    me = lax.axis_index(axis)
    for s, ref in enumerate(square_refs):
        square_ref[me ^ s] = ref[...]
    square = sum(square_ref[k] for k in range(parts))
    weight = 1.0 / (1.0 + 4.0 * (square / comps))
    rows = aligned_ref.shape[0]
    width, frames = weighted_ref.shape
    weighted_ref[0:rows, :] = aligned_ref[...] * weight
    tail = lax.broadcasted_iota(jnp.int32, (width - rows, frames), 0)
    weighted_ref[rows:, :] = jnp.where(tail == 0, weight, 0.0)
    weighted = weighted_ref[...]
    high = weighted.astype(jnp.bfloat16)
    low = (weighted - high.astype(jnp.float32)).astype(jnp.bfloat16)
    member = member_ref[...]
    over_frames = (((1,), (1,)), ((), ()))
    summed_ref[...] = lax.dot_general(
        member, high, over_frames, preferred_element_type=jnp.float32
    ) + lax.dot_general(member, low, over_frames, preferred_element_type=jnp.float32)
    here = lax.axis_index(owners_axis)
    for k, out_ref in enumerate(out_refs):
        states = out_ref.shape[1]
        for s in range(out_ref.shape[0]):
            at = pl.multiple_of((here ^ (2 * s + k)) * states, 8)
            out_ref[s] = summed_ref[pl.ds(at, states), :]


def gather(member, aligned, squares, axis, owners_axis, comps):
    micro, frames = member.shape
    owners = lax.axis_size(owners_axis)
    rows = aligned.shape[0]
    width = round_up(rows + 1, 128)
    return pl.pallas_call(
        functools.partial(gather_kernel, axis, owners_axis, comps, len(squares)),
        out_shape=[jax.ShapeDtypeStruct((owners // 2, micro // owners, width), jnp.float32)] * 2,
        scratch_shapes=[
            pltpu.VMEM((len(squares), 1, frames), jnp.float32),
            pltpu.VMEM((width, frames), jnp.float32),
            pltpu.VMEM((micro, width), jnp.float32),
        ],
        compiler_params=pltpu.CompilerParams(vmem_limit_bytes=16 * MIB),
        name="gather",
    )(member, aligned, *squares)


def merge_kernel(mine_ref, other_ref, *out_refs):
    for s, out_ref in enumerate(out_refs):
        out_ref[...] = mine_ref[s] + other_ref[s]


def merge(mine, other):
    count = mine.shape[0]
    return pl.pallas_call(
        merge_kernel,
        out_shape=[jax.ShapeDtypeStruct(mine.shape[1:], jnp.float32)] * count,
        compiler_params=pltpu.CompilerParams(vmem_limit_bytes=8 * MIB),
        name="merge",
    )(mine, other)


def update_kernel(axis, quarter, centroids_ref, *refs):
    piece_refs = refs[:-3]
    out_ref, occupancy_ref, pieces_ref = refs[-3:]
    parts = len(piece_refs)
    dims, states, res_count = centroids_ref.shape
    me = lax.axis_index(axis)
    for s, ref in enumerate(piece_refs):
        pieces_ref[me ^ s] = ref[...]
    occupancy = pieces_ref[0][:, dims * quarter : dims * quarter + 1]
    row = lax.broadcasted_iota(jnp.int32, (states, states), 0)
    column = lax.broadcasted_iota(jnp.int32, (states, states), 1)
    occupancy_ref[...] = jnp.sum(jnp.where(row == column, occupancy, 0.0), axis=0, keepdims=True)
    divisor = prior_weight + occupancy
    for c in range(dims):
        rows = centroids_ref[c]
        rows = rows - jnp.sum(rows, axis=1, keepdims=True) / res_count
        for z in range(parts):
            low, high = z * quarter, min((z + 1) * quarter, res_count)
            summed = pieces_ref[z][:, c * quarter : c * quarter + high - low]
            out_ref[c, :, low:high] = (prior_weight * rows[:, low:high] + summed) / divisor


def update(centroids, pieces, axis, quarter):
    dims, states, res_count = centroids.shape
    return pl.pallas_call(
        functools.partial(update_kernel, axis, quarter),
        out_shape=[
            jax.ShapeDtypeStruct((dims, states, res_count), jnp.float32),
            jax.ShapeDtypeStruct((1, states), jnp.float32),
        ],
        scratch_shapes=[pltpu.VMEM((len(pieces),) + pieces[0].shape, jnp.float32)],
        compiler_params=pltpu.CompilerParams(vmem_limit_bytes=8 * MIB),
        name="update",
    )(centroids, *pieces)


def swap(value, axis, step):
    size = lax.axis_size(axis)
    return lax.ppermute(value, axis, [(i, i ^ step) for i in range(size)])


def gathered(value, axis, first=1):
    steps = range(first, lax.axis_size(axis), first)
    return [value] + [swap(value, axis, s) for s in steps]


def local(coords, centroids, assignment, home_row, pair_index, mean_dist, tica_weight):
    comps = tica_weight.shape[1]
    parts = lax.axis_size("pairs")
    coords = jnp.transpose(coords, (1, 2, 0))
    centroids = jnp.transpose(centroids, (1, 0, 2))
    quarter = round_up(-(-coords.shape[1] // parts), 8)

    other = swap(centroids, "frames", 1)
    positions, unit = split_coords(coords)
    positions, both = lax.optimization_barrier((positions, jnp.stack([centroids, other])))
    refs = gathered(both, "frames", 2)
    partial = project(
        positions, unit, coords.shape[1], pair_index, mean_dist[None, :], tica_weight.T, "pairs"
    )
    partial, refs = lax.optimization_barrier((partial, refs))
    received = [swap(partial[s], "pairs", s) for s in reversed(range(1, parts))]
    member, aligned, received = lax.optimization_barrier(
        (
            *align(coords, assignment, home_row, refs, "frames", "pairs", quarter),
            received,
        )
    )
    tica, square = finish([partial[0], *received], comps // parts, coords.shape[2])
    squares = gathered(square, "pairs")
    mine, other = gather(member, aligned, squares, "pairs", "frames", comps)
    sums = merge(mine, swap(other, "frames", 1))
    total = sums[0]
    for s in reversed(range(1, len(sums))):
        total = total + swap(sums[s], "frames", 2 * s)
    new_centroids, occupancy = update(centroids, gathered(total, "pairs"), "pairs", quarter)
    return (tica.T, jnp.transpose(new_centroids, (1, 0, 2)), occupancy[0])


def solution(mesh):
    in_specs = (
        P("frames", None, None),
        P("frames", None, None),
        P("frames"),
        P(),
        P(None, "pairs"),
        P("pairs"),
        P("pairs", None),
    )
    out_specs = (P("frames", "pairs"), P("frames", None, None), P("frames"))
    return jax.shard_map(local, mesh=mesh, in_specs=in_specs, out_specs=out_specs, check_vma=False)
```
